32 devices in a mesh: replica: 2 (over y), fsdp: 16 (over z, x, core).
Axes of the slice: x: 2, y: 2, z: 4, core: 2. Of those that a mesh axis runs over, the one named last changes fastest.
Arguments:
- hidden_states: bfloat16 [8192, 8192], P(('replica', 'fsdp')), may hold values from -6 to 6
- key_weight: bfloat16 [8192, 1024], P('fsdp'), may hold values from -0.13258252 to 0.13258252
- previous_peak: float32 [1], replicated, may hold values from 0.088388346 to 0.12705825
- key_cotangent: bfloat16 [8192, 1024], P(('replica', 'fsdp')), may hold values from -6 to 6
Outputs:
- projected_keys: bfloat16 [8192, 1024], P(('replica', 'fsdp'))
- input_gradient: bfloat16 [8192, 8192], P(('replica', 'fsdp'))
- weight_gradient: bfloat16 [8192, 1024], P('fsdp')
- peak_ratio: float32 [1], replicated
The draws below stay inside these ranges and needn't reach their ends.
All inputs are finite; a program needn't handle non-finite values.
Results may differ from the reference program's by a relative error of at most 0.025.
Values may be sent and summed in bfloat16 or wider, within the bound.
No kernel may reach another device: no remote copies, remote signals or barrier semaphores. Data moves between devices by JAX's collectives and lax.ppermute only.
A program may use at most 128 MiB of HBM per device.

```python
import jax
import jax.numpy as jnp
from jax import lax

D = 8192
KV = 1024
TOK_DEV = 256
TOKENS = 8192
N_REPLICA = 2
N_FSDP = 16


def draw_key_weight(key, part):
    key = jax.random.fold_in(key, 7)
    rising = 1.0 + 2.0 * jnp.arange(D, dtype=jnp.float32)[:, None] / (D - 1)
    base = jax.random.truncated_normal(key, -4.0, 4.0, (D, KV), jnp.float32)
    return (base * rising * D ** (-0.5)).astype(jnp.bfloat16)


def with_spikes(array, key, source, target, blocks, factor):
    def block_of(axis_at):
        return (jnp.arange(array.shape[axis_at]) // (array.shape[axis_at] // blocks)).reshape((-1,) + (1,) * (array.ndim - 1 - axis_at))

    one_side = jax.random.permutation(key, blocks)[block_of(target)]
    second = (block_of(target) + blocks // 2) % blocks
    return jnp.where((block_of(source) == one_side) | (block_of(source) == second), factor * array, array)


def levels(key, shape, pieces, least, largest):
    def one(dim, parts):
        heights = jax.random.uniform(jax.random.fold_in(jax.random.fold_in(key, 6), dim), (parts,), jnp.float32, least / len(pieces), largest / len(pieces))
        return jnp.repeat(jnp.exp(heights), shape[dim] // parts).reshape((-1,) + (1,) * (len(shape) - dim - 1))

    gain = one(*pieces[0])
    for cut in pieces[1:]:
        gain = gain * one(*cut)
    return gain


def noise(stream_key, dims, spread, reach, shards=(), kind=jnp.bfloat16):
    gain = levels(stream_key, dims, shards, -0.22, 0.18) if shards else 1.0
    result = jax.random.normal(stream_key, dims, jnp.float32) * spread * gain
    return jnp.minimum(jnp.maximum(result, -reach), reach).astype(kind)


def noise_with(stream_key, dims, scale, reach, shards, heavy, held_as=jnp.bfloat16):
    drawn = scale * jax.random.normal(stream_key, dims, jnp.float32)
    if shards:
        drawn = drawn * levels(stream_key, dims, shards, -0.22, 0.18)
    return jnp.clip(with_spikes(drawn, jax.random.fold_in(stream_key, 3), *heavy), -reach, reach).astype(held_as)


def setup_inputs(seed: int = 0) -> dict:
    seeds = jax.random.split(jax.random.key(seed), 5)
    hidden_states = noise_with(seeds[0], (TOKENS, D), 1.0, 6.0, ((0, 32),), (0, 1, 32, 2.75))
    key_weight = draw_key_weight(jax.random.fold_in(seeds[4], 71), 0)
    previous_peak = jnp.clip(jax.random.uniform(seeds[2], (1,), jnp.float32, 0.088388346, 0.12705825), 0.088388346, 0.12705825)
    key_cotangent = noise(seeds[3], (TOKENS, KV), 1.0, 6.0, ((0, 32),))
    return dict(hidden_states=hidden_states, key_weight=key_weight, previous_peak=previous_peak, key_cotangent=key_cotangent)


def quantize(weight, limit):
    return jnp.clip(weight.astype(jnp.float32) * (448.0 / limit), -448.0, 448.0).astype(jnp.bfloat16)


def reference(hidden_states, key_weight, previous_peak, key_cotangent):
    limit = previous_peak[0]
    unscale = limit / 448.0
    codes = quantize(key_weight, limit)
    projected_keys = (jnp.dot(hidden_states, codes, preferred_element_type=jnp.float32) * unscale).astype(jnp.bfloat16)
    input_gradient = (jnp.dot(key_cotangent, codes.T, preferred_element_type=jnp.float32) * unscale).astype(jnp.bfloat16)
    blocks_x = hidden_states.reshape(N_REPLICA, N_FSDP, TOK_DEV, D)
    blocks_g = key_cotangent.reshape(N_REPLICA, N_FSDP, TOK_DEV, KV)

    def device_step(acc, pair):
        term = jnp.dot(pair[0].T, pair[1], preferred_element_type=jnp.float32).astype(jnp.bfloat16)
        term = lax.optimization_barrier(term)
        return acc + term.astype(jnp.float32), None

    def replica_step(total, pair):
        group, unused = lax.scan(device_step, jnp.zeros((D, KV), jnp.float32), pair)
        rounded = lax.optimization_barrier(group.astype(jnp.bfloat16))
        return total + rounded.astype(jnp.float32), None

    total, unused = lax.scan(replica_step, jnp.zeros((D, KV), jnp.float32), (blocks_x, blocks_g))
    weight_gradient = (total * (TOKENS ** -0.5)).astype(jnp.bfloat16)
    peak = jnp.max(jnp.abs(key_weight.astype(jnp.float32)))
    peak_ratio = (peak / limit).reshape(1)
    return projected_keys, input_gradient, weight_gradient, peak_ratio
```

```python
import functools

import jax
import jax.numpy as jnp
from jax import lax
from jax.experimental import pallas as pl
from jax.experimental.pallas import tpu as pltpu
from jax.sharding import Mesh
from jax.sharding import PartitionSpec as P

ANY = pl.BlockSpec(memory_space=pl.ANY)
SMEM = pl.BlockSpec(memory_space=pltpu.SMEM)
VMEM = pl.BlockSpec(memory_space=pltpu.VMEM)
PARAMS = pltpu.CompilerParams(vmem_limit_bytes=63 * 2**20)
CHEAP = pl.CostEstimate(flops=1, bytes_accessed=1, transcendentals=0)
F32, BF16 = jnp.float32, jnp.bfloat16


def quantize(weight, limit):
    return jnp.clip(weight.astype(F32) * (448.0 / limit), -448.0, 448.0).astype(BF16)


def swap(block, axis, mask=1):
    size = lax.axis_size(axis)
    return lax.ppermute(block, axis, [(i, i ^ mask) for i in range(size)])


def run(copies):
    for copy in copies:
        copy.start()
    for copy in copies:
        copy.wait()


def pack(core, hidden, rows, nz):
    tokens = hidden.shape[0]
    half = rows // 2
    group, blocks = 8, nz * 2

    def kernel(core_ref, hidden_ref, group_ref, other_ref, sem):
        copies = []
        for d in range(group):
            for k in range(nz):
                start = (k * 4 + d % 4) * rows + (d // 4) * half
                copies.append(
                    pltpu.make_async_copy(
                        hidden_ref.at[:, pl.ds(start, half)],
                        group_ref.at[d, :, pl.ds(k * half, half)],
                        sem.at[len(copies)],
                    )
                )
        for b in range(blocks):
            start = pl.multiple_of((b * 2 + 1 - core_ref[0]) * rows, rows)
            copies.append(
                pltpu.make_async_copy(
                    hidden_ref.at[:, pl.ds(start, rows)], other_ref.at[b], sem.at[len(copies)]
                )
            )
        run(copies)

    return pl.pallas_call(
        kernel,
        out_shape=[
            jax.ShapeDtypeStruct((group, tokens, nz * half), BF16),
            jax.ShapeDtypeStruct((blocks, tokens, rows), BF16),
        ],
        in_specs=[SMEM, ANY],
        out_specs=[VMEM, VMEM],
        scratch_shapes=[pltpu.SemaphoreType.DMA((group * nz + blocks,))],
        compiler_params=PARAMS,
        name="pack",
    )(core, hidden)


def weight_terms(slots, swapped, cotangents, tiles, state):
    sources, tokens, width = swapped.shape
    features = cotangents[0].shape[1]
    count = len(tiles)
    tile = width // 4

    def kernel(slots_ref, swapped_ref, *refs):
        cots_ref, refs = refs[:2], refs[2 + len(state) :]
        out_ref, lhs, rhs, out, sem, out_sem = refs
        copies = []
        for s in range(sources):
            place = pl.ds(pl.multiple_of(slots_ref[s] * tokens, tokens), tokens)
            source = cots_ref[s // 4].at[pl.ds(s % 4 * tokens, tokens)]
            copies.append(pltpu.make_async_copy(source, rhs.at[place], sem.at[count, s]))
        for i, t in enumerate(tiles):
            at = pl.ds(t * tile, tile)
            for s in range(sources):
                place = pl.ds(s * tokens, tokens)
                copies.append(
                    pltpu.make_async_copy(swapped_ref.at[s, :, at], lhs.at[i, place], sem.at[i, s])
                )
        for copy in copies:
            copy.start()
        stores = []
        for i, t in enumerate(tiles):
            for copy in copies[(i + 1 if i else 0) * sources : (i + 2) * sources]:
                copy.wait()
            out[i] = lax.dot_general(
                lhs[i], rhs[...], (((0,), (0,)), ((), ())), preferred_element_type=F32
            ).astype(BF16)
            target = out_ref.at[pl.ds(t * tile, tile)]
            stores.append(pltpu.make_async_copy(out.at[i], target, out_sem.at[i]))
            stores[-1].start()
        for copy in stores:
            copy.wait()

    return pl.pallas_call(
        kernel,
        out_shape=jax.ShapeDtypeStruct((width, features), BF16),
        in_specs=[SMEM] + [ANY] * (3 + len(state)),
        out_specs=ANY,
        input_output_aliases={4: 0} if state else {},
        scratch_shapes=[
            pltpu.VMEM((count, sources * tokens, tile), BF16),
            pltpu.VMEM((sources * tokens, features), BF16),
            pltpu.VMEM((count, tile, features), BF16),
            pltpu.SemaphoreType.DMA((count + 1, sources)),
            pltpu.SemaphoreType.DMA((count,)),
        ],
        cost_estimate=CHEAP,
        compiler_params=PARAMS,
        name="weight_terms",
    )(slots, swapped, *cotangents, *state)


def consume(where, scale, hidden, other, cotangents, units, state, arrived, last=False):
    tokens, width = hidden.shape
    rows, features = other.shape[2], cotangents[0].shape[1]
    half = rows // 2
    count = len(units)
    extra = len(arrived[1]) if arrived else 0
    chunks = [min(4, count - i) for i in range(0, count, 4)]
    arrays = []
    for array, _, _ in units:
        if not any(array is known for known in arrays):
            arrays.append(array)

    def kernel(where_ref, scale_ref, hidden_ref, other_ref, *refs):
        cots_ref, refs = refs[:2], refs[2:]
        array_refs, refs = refs[: len(arrays)], refs[len(arrays) :]
        if state:
            totals_ref, refs = refs[:2], refs[3:]
        arrived_refs, refs = refs[: (extra + 3) // 4], refs[(extra + 3) // 4 :]
        total_refs, gradient_ref, away_refs, refs = refs[:2], refs[2], refs[3 : 3 + len(chunks)], refs[3 + len(chunks) :]
        hid, cot, wgt, acc, prior, near, far, held, sent, sem, cot_sem, out_sem, near_sem, far_sem = refs
        place = functools.partial(unit_columns, where_ref, rows)
        early = []
        for s in range(2):
            span = pl.ds(s * tokens, tokens)
            source = cots_ref[s].at[pl.ds(0, tokens)]
            early.append(pltpu.make_async_copy(source, cot.at[span], cot_sem.at[s]))
        for copy in early:
            copy.start()
        loads = []
        for b, (array, row, (k, side, part)) in enumerate(units):
            ref = [r for r, known in zip(array_refs, arrays) if known is array][0]
            at = pl.multiple_of((1 - where_ref[2] if part else where_ref[2]) * half, half)
            if len(array.shape) == 3:
                source = ref.at[where_ref[3] ^ k]
            else:
                source = ref.at[pl.ds(at if row is None else row, half)]
            block = (where_ref[3] ^ k) * 2 + (1 - where_ref[1] if side else where_ref[1])
            pairs = [
                (source, wgt.at[b]),
                (hidden_ref.at[:, place((k, side, part), 0)], hid.at[b, pl.ds(0, tokens)]),
                (other_ref.at[block, :, pl.ds(at, half)], hid.at[b, pl.ds(tokens, tokens)]),
            ]
            loads.append([pltpu.make_async_copy(f, t, sem.at[i, b]) for i, (f, t) in enumerate(pairs)])
            for copy in loads[-1]:
                copy.start()
        before = []
        for i, ref in enumerate(arrived_refs):
            size = min(4, extra - 4 * i)
            before.append(pltpu.make_async_copy(ref, held.at[pl.ds(4 * i, size)], cot_sem.at[4 + i]))
        if state:
            for s in range(2):
                span = pl.ds(s * tokens, tokens)
                before.append(pltpu.make_async_copy(totals_ref[s], prior.at[span], cot_sem.at[2 + s]))
        for copy in before:
            copy.start()
        for copy in early:
            copy.wait()
        acc[...] = jnp.zeros_like(acc)

        def step(b, carry):
            for i, ref in enumerate((wgt.at[b], hid.at[b, pl.ds(0, tokens)], hid.at[b, pl.ds(0, tokens)])):
                pltpu.make_async_copy(ref, ref, sem.at[i, b]).wait()
            weight = wgt[b]
            acc[...] += jnp.dot(hid[b], weight, preferred_element_type=F32)
            product = (
                lax.dot_general(
                    cot[...], weight, (((1,), (1,)), ((), ())), preferred_element_type=F32
                )
                * scale_ref[0]
            ).astype(BF16)
            near[b] = product[:tokens]
            far[b] = product[tokens:]
            return carry

        lax.fori_loop(0, count, step, 0)
        late = [
            pltpu.make_async_copy(far.at[pl.ds(4 * i, size)], away_refs[i], far_sem.at[i])
            for i, size in enumerate(chunks)
        ]
        for b, (_, _, unit) in enumerate(units):
            late.append(
                pltpu.make_async_copy(near.at[b], gradient_ref.at[:, place(unit, 0)], near_sem.at[b])
            )
        for copy in late:
            copy.start()
        for copy in before:
            copy.wait()
        if state:
            acc[...] += prior[...]
        sums = [acc.at[pl.ds(s * tokens, tokens)] for s in range(2)]
        if last:
            sent[...] = acc[pl.ds(tokens, tokens)].astype(BF16)
            sums[1] = sent
        end = [pltpu.make_async_copy(sums[s], total_refs[s], out_sem.at[s]) for s in range(2)]
        for e in range(extra):
            columns = place(arrived[1][e], 1)
            end.append(
                pltpu.make_async_copy(held.at[e], gradient_ref.at[:, columns], out_sem.at[2 + e])
            )
        for copy in end:
            copy.start()
        for copy in late + end:
            copy.wait()

    sums = jax.ShapeDtypeStruct((tokens, features), F32)
    operands = [where, scale, hidden, other, *cotangents, *arrays, *state]
    if arrived:
        operands += arrived[0]
    return pl.pallas_call(
        kernel,
        out_shape=[
            sums,
            jax.ShapeDtypeStruct(sums.shape, BF16) if last else sums,
            jax.ShapeDtypeStruct((tokens, width), BF16),
            *[jax.ShapeDtypeStruct((size, tokens, half), BF16) for size in chunks],
        ],
        in_specs=[SMEM, SMEM] + [ANY] * (len(operands) - 2),
        out_specs=[ANY] * (3 + len(chunks)),
        input_output_aliases=(
            {6 + len(arrays) + i: i for i in (0, 2) + (() if last else (1,))} if state else {}
        ),
        scratch_shapes=[
            pltpu.VMEM((count, 2 * tokens, half), BF16),
            pltpu.VMEM((2 * tokens, features), BF16),
            pltpu.VMEM((count, half, features), BF16),
            pltpu.VMEM((2 * tokens, features), F32),
            pltpu.VMEM((2 * tokens, features) if state else (8, 128), F32),
            pltpu.VMEM((count, tokens, half), BF16),
            pltpu.VMEM((count, tokens, half), BF16),
            pltpu.VMEM((max(extra, 1), tokens, half), BF16),
            pltpu.VMEM((tokens, features) if last else (16, 128), BF16),
            pltpu.SemaphoreType.DMA((3, count)),
            pltpu.SemaphoreType.DMA((4 + (extra + 3) // 4,)),
            pltpu.SemaphoreType.DMA((2 + extra,)),
            pltpu.SemaphoreType.DMA((count,)),
            pltpu.SemaphoreType.DMA((len(chunks),)),
        ],
        cost_estimate=CHEAP,
        compiler_params=PARAMS,
        name="consume",
    )(*operands)


def unit_columns(where_ref, rows, unit, core):
    k, side, part = unit
    half = rows // 2
    x = 1 - where_ref[1] if side else where_ref[1]
    c = 1 - where_ref[0] if core else where_ref[0]
    r = 1 - where_ref[2] if part else where_ref[2]
    at = (((where_ref[3] ^ k) * 2 + x) * 2 + c) * rows + r * half
    return pl.ds(pl.multiple_of(at, half), half)


def finish(where, scale, gradient, arrived, units, sums, shares):
    half, features = shares[0].shape
    counts = [len(some) for some in units]

    def kernel(where_ref, scale_ref, *refs):
        arrived_refs, refs = refs[: len(units)], refs[len(units) :]
        a_ref, b_ref, mine_ref, theirs_ref, _, gradient_ref, keys_ref, weight_ref, sem = refs
        copies = []
        for ref, some in zip(arrived_refs, units):
            for e, unit in enumerate(some):
                columns = unit_columns(where_ref, 2 * half, unit, 1)
                copies.append(
                    pltpu.make_async_copy(ref.at[e], gradient_ref.at[:, columns], sem.at[len(copies)])
                )
        for copy in copies:
            copy.start()
        at = pl.multiple_of(where_ref[2] * half, half)
        weight_ref[pl.ds(at, half), :] = mine_ref[...]
        weight_ref[pl.ds(half - at, half), :] = theirs_ref[pl.ds(0, half), :]
        keys_ref[...] = ((a_ref[...] + b_ref[...].astype(F32)) * scale_ref[0]).astype(BF16)
        for copy in copies:
            copy.wait()

    return pl.pallas_call(
        kernel,
        out_shape=[
            jax.ShapeDtypeStruct(gradient.shape, BF16),
            jax.ShapeDtypeStruct(sums[0].shape, BF16),
            jax.ShapeDtypeStruct((2 * half, features), BF16),
        ],
        in_specs=[SMEM, SMEM] + [VMEM] * (len(units) + 4) + [ANY],
        out_specs=[ANY, VMEM, VMEM],
        input_output_aliases={len(units) + 6: 0},
        scratch_shapes=[pltpu.SemaphoreType.DMA((sum(counts),))],
        compiler_params=PARAMS,
        name="finish",
    )(where, scale, *arrived, *sums, *shares, gradient)


def body(hidden, key_weight, previous_peak, cotangent):
    limit = previous_peak[0]
    unscale = limit / 448.0
    scale = unscale.reshape(1)
    tokens = hidden.shape[0]
    rows = key_weight.shape[0]
    r, z, x, c = (lax.axis_index(name) for name in ("replica", "z", "x", "core"))
    where = jnp.stack([c, x, r, z]).astype(jnp.int32)
    nz = lax.axis_size("z")
    token_count = tokens * lax.axis_size(("replica", "z", "x", "core"))

    codes = quantize(key_weight, limit)
    half = rows // 2
    own = lax.dynamic_slice_in_dim(codes, r * half, half, 0)
    rest = lax.dynamic_slice_in_dim(codes, (1 - r) * half, half, 0)
    hidden, own, rest = lax.optimization_barrier((hidden, own, rest))
    mine = lax.all_gather(own, "z", axis=0)
    rest, mine = lax.optimization_barrier((rest, mine))
    theirs = lax.all_gather(rest, "z", axis=0)

    cots = [swap(cotangent, "x"), swap(cotangent, "replica"), swap(cotangent, ("replica", "x"), 3)]
    for_group, for_other = pack(where, hidden, rows, nz)
    for_group, *cots = lax.optimization_barrier((for_group, *cots))
    swapped = lax.all_to_all(for_group, ("replica", "x", "core"), 0, 0, tiled=True)
    peaks = jnp.max(jnp.abs(key_weight), axis=0, keepdims=True)
    peaks = jnp.broadcast_to(peaks, (16, peaks.shape[1]))
    for k in (1, 2):
        peaks = jnp.maximum(peaks, swap(peaks, "z", k))
    cots = jnp.concatenate([cotangent, *cots], axis=0)
    cots, peaks = lax.optimization_barrier((cots, peaks))
    cots = [cots, swap(cots, "core")]
    slots = [
        ((r ^ dr) * 2 + (x ^ dx)) * 2 + (c ^ dc) for dc in (0, 1) for dr in (0, 1) for dx in (0, 1)
    ]
    slots = jnp.stack(slots).astype(jnp.int32)
    other = swap(for_other, "core")

    parts = [own] + [lax.dynamic_index_in_dim(mine, z ^ k, keepdims=False) for k in (1, 2, 3)]
    parts[3] = jnp.concatenate([parts[3], peaks])
    swapped, other = lax.optimization_barrier((swapped, other))
    stage = functools.partial(consume, where, scale, hidden, other, [cotangent, cots[1]])

    cots[1], *parts = lax.optimization_barrier((cots[1], *parts))
    side0 = swap(parts[0], "x")
    term = weight_terms(slots, swapped, cots, (0, 1, 2, 3), [])

    term, side0, theirs, *parts = lax.optimization_barrier((term, side0, theirs, *parts))
    total = lax.psum_scatter(term, "z", scatter_dimension=0, tiled=True).astype(F32)
    side1, other0 = swap(parts[1], "x"), swap(side0, "replica")
    units = [(codes, None, (0, 0, part)) for part in (0, 1)]
    units += [(block, None, (k, 0, part)) for part, block in enumerate((mine, theirs)) for k in (1, 2, 3)]
    *state, away0, away1 = stage(units, [], None)
    arrived = ([swap(away0, "core"), swap(away1, "core")], [unit for _, _, unit in units])

    side1, other0, *rest = lax.optimization_barrier((side1, other0, *state, *parts))
    state, parts = rest[:3], rest[3:]
    side2, other1 = swap(parts[2], "x"), swap(side1, "replica")
    units = [(side0, 0, (0, 1, 0)), (other0, 0, (0, 1, 1)), (side1, 0, (1, 1, 0))]
    *state, away = stage(units, state, None)
    late = [swap(away, "core")]
    late_units = [[unit for _, _, unit in units]]

    side2, other1, *rest = lax.optimization_barrier((side2, other1, *state, *parts))
    state, parts = rest[:3], rest[3:]
    side3, other2 = swap(parts[3], "x"), swap(side2, "replica")

    side3, other2, *state = lax.optimization_barrier((side3, other2, *state))
    other3 = swap(side3, "replica")
    units = [(other1, 0, (1, 1, 1)), (side2, 0, (2, 1, 0)), (other2, 0, (2, 1, 1)), (side3, 0, (3, 1, 0))]
    *state, away = stage(units, state, arrived)
    late.append(swap(away, "core"))
    late_units.append([unit for _, _, unit in units])

    peak = jnp.maximum(jnp.max(peaks), jnp.max(side3[half:]))
    peak = jnp.full((8, 128), peak.astype(F32))
    peak = jnp.maximum(peak, swap(peak, "core"))
    peak_ratio = (peak[0, 0] / limit).reshape(1)

    share = (total * token_count ** (-0.5)).astype(BF16)
    other_share = swap(jnp.pad(share, ((0, 16), (0, 0))), "replica")
    other3, peak_ratio, *state = lax.optimization_barrier((other3, peak_ratio, *state))
    *state, away = stage([(other3, 0, (3, 1, 1))], state, None, last=True)
    late.append(swap(away, "core"))
    late_units.append([(3, 1, 1)])
    sums = [state[0], swap(state[1], "core")]
    input_gradient, projected_keys, weight_gradient = finish(
        where, scale, state[2], late, late_units, sums, [share, other_share]
    )
    return (projected_keys, input_gradient, weight_gradient, peak_ratio)


def plain(hidden_states, key_weight, previous_peak, key_cotangent):
    names = ("replica", "x", "core")
    limit = previous_peak[0]
    unscale = limit / 448.0
    tokens, width = hidden_states.shape
    rows, features = key_weight.shape
    replicas = lax.axis_size("replica")
    nz, nx, nc = lax.axis_size("z"), lax.axis_size("x"), lax.axis_size("core")
    part = rows // replicas
    group = replicas * nx * nc
    split = hidden_states.reshape(tokens, nz, nx, nc, replicas, part)
    split = split.transpose(4, 2, 3, 0, 1, 5).reshape(group, tokens, nz * part)
    swapped = lax.all_to_all(split, names, 0, 0, tiled=True)
    cotangents = lax.all_gather(key_cotangent, names, axis=0, tiled=True)
    peak = lax.pmax(jnp.max(jnp.abs(key_weight.astype(F32))), ("z", "x", "core"))
    half = lax.dynamic_slice_in_dim(key_weight, lax.axis_index("replica") * part, part, 0)
    gathered = lax.all_gather(
        quantize(half, limit), ("z", "x", "core", "replica"), axis=0, tiled=True
    )
    keys_sum = jnp.dot(hidden_states, gathered, preferred_element_type=F32)
    grad_sum = lax.dot_general(
        key_cotangent, gathered, (((1,), (1,)), ((), ())), preferred_element_type=F32
    )
    term = lax.dot_general(
        swapped.reshape(group * tokens, nz * part),
        cotangents,
        (((0,), (0,)), ((), ())),
        preferred_element_type=F32,
    ).astype(BF16)
    total = lax.psum_scatter(term, "z", scatter_dimension=0, tiled=True).astype(F32)
    token_count = tokens * replicas * nz * nx * nc
    share = (total * token_count ** (-0.5)).astype(BF16)
    weight_gradient = lax.all_gather(share, "replica", axis=0, tiled=True)
    return (
        (keys_sum * unscale).astype(BF16),
        (grad_sum * unscale).astype(BF16),
        weight_gradient,
        (peak / limit).reshape(1),
    )


def solution(mesh):
    replicas, shards = mesh.shape["replica"], mesh.shape["fsdp"]
    grid = Mesh(mesh.devices.reshape(replicas, shards // 4, 2, 2), ("replica", "z", "x", "core"))
    fsdp = ("z", "x", "core")
    every = ("replica",) + fsdp
    in_specs = (P(every, None), P(fsdp, None), P(), P(every, None))
    out_specs = (P(every, None), P(every, None), P(fsdp, None), P())
    run = body if replicas == 2 and shards == 16 else plain
    return jax.shard_map(run, mesh=grid, in_specs=in_specs, out_specs=out_specs, check_vma=False)
```

```python
import functools

import jax
import jax.numpy as jnp
from jax import lax
from jax.experimental import pallas as pl
from jax.experimental.pallas import tpu as pltpu
from jax.sharding import Mesh
from jax.sharding import PartitionSpec as P

ANY = pl.BlockSpec(memory_space=pl.ANY)
SMEM = pl.BlockSpec(memory_space=pltpu.SMEM)
VMEM = pl.BlockSpec(memory_space=pltpu.VMEM)
PARAMS = pltpu.CompilerParams(vmem_limit_bytes=63 * 2**20)
CHEAP = pl.CostEstimate(flops=1, bytes_accessed=1, transcendentals=0)
F32, BF16 = jnp.float32, jnp.bfloat16


def quantize(weight, limit):
    return jnp.clip(weight.astype(F32) * (448.0 / limit), -448.0, 448.0).astype(BF16)


def swap(block, axis, mask=1):
    size = lax.axis_size(axis)
    return lax.ppermute(block, axis, [(i, i ^ mask) for i in range(size)])


def run(copies):
    for copy in copies:
        copy.start()
    for copy in copies:
        copy.wait()


def pack(core, hidden, rows, nz):
    tokens = hidden.shape[0]
    half = rows // 2
    group, blocks = 8, nz * 2

    def kernel(core_ref, hidden_ref, group_ref, other_ref, sem):
        copies = []
        for d in range(group):
            for k in range(nz):
                start = (k * 4 + d % 4) * rows + (d // 4) * half
                copies.append(
                    pltpu.make_async_copy(
                        hidden_ref.at[:, pl.ds(start, half)],
                        group_ref.at[d, :, pl.ds(k * half, half)],
                        sem.at[len(copies)],
                    )
                )
        for b in range(blocks):
            start = pl.multiple_of((b * 2 + 1 - core_ref[0]) * rows, rows)
            copies.append(
                pltpu.make_async_copy(
                    hidden_ref.at[:, pl.ds(start, rows)], other_ref.at[b], sem.at[len(copies)]
                )
            )
        run(copies)

    return pl.pallas_call(
        kernel,
        out_shape=[
            jax.ShapeDtypeStruct((group, tokens, nz * half), BF16),
            jax.ShapeDtypeStruct((blocks, tokens, rows), BF16),
        ],
        in_specs=[SMEM, ANY],
        out_specs=[VMEM, VMEM],
        scratch_shapes=[pltpu.SemaphoreType.DMA((group * nz + blocks,))],
        compiler_params=PARAMS,
        name="pack",
    )(core, hidden)


def weight_terms(slots, swapped, cotangents, tiles, state):
    sources, tokens, width = swapped.shape
    features = cotangents[0].shape[1]
    count = len(tiles)
    tile = width // 4

    def kernel(slots_ref, swapped_ref, *refs):
        cots_ref, refs = refs[:2], refs[2 + len(state) :]
        out_ref, lhs, rhs, out, sem, out_sem = refs
        copies = []
        for s in range(sources):
            place = pl.ds(pl.multiple_of(slots_ref[s] * tokens, tokens), tokens)
            source = cots_ref[s // 4].at[pl.ds(s % 4 * tokens, tokens)]
            copies.append(pltpu.make_async_copy(source, rhs.at[place], sem.at[count, s]))
        for i, t in enumerate(tiles):
            at = pl.ds(t * tile, tile)
            for s in range(sources):
                place = pl.ds(s * tokens, tokens)
                copies.append(
                    pltpu.make_async_copy(swapped_ref.at[s, :, at], lhs.at[i, place], sem.at[i, s])
                )
        for copy in copies:
            copy.start()
        stores = []
        for i, t in enumerate(tiles):
            for copy in copies[(i + 1 if i else 0) * sources : (i + 2) * sources]:
                copy.wait()
            out[i] = lax.dot_general(
                lhs[i], rhs[...], (((0,), (0,)), ((), ())), preferred_element_type=F32
            ).astype(BF16)
            target = out_ref.at[pl.ds(t * tile, tile)]
            stores.append(pltpu.make_async_copy(out.at[i], target, out_sem.at[i]))
            stores[-1].start()
        for copy in stores:
            copy.wait()

    return pl.pallas_call(
        kernel,
        out_shape=jax.ShapeDtypeStruct((width, features), BF16),
        in_specs=[SMEM] + [ANY] * (3 + len(state)),
        out_specs=ANY,
        input_output_aliases={4: 0} if state else {},
        scratch_shapes=[
            pltpu.VMEM((count, sources * tokens, tile), BF16),
            pltpu.VMEM((sources * tokens, features), BF16),
            pltpu.VMEM((count, tile, features), BF16),
            pltpu.SemaphoreType.DMA((count + 1, sources)),
            pltpu.SemaphoreType.DMA((count,)),
        ],
        cost_estimate=CHEAP,
        compiler_params=PARAMS,
        name="weight_terms",
    )(slots, swapped, *cotangents, *state)


def consume(where, scale, hidden, other, cotangents, units, state, arrived, last=False):
    tokens, width = hidden.shape
    rows, features = other.shape[2], cotangents[0].shape[1]
    half = rows // 2
    count = len(units)
    extra = len(arrived[1]) if arrived else 0
    chunks = [min(4, count - i) for i in range(0, count, 4)]
    arrays = []
    for array, _, _ in units:
        if not any(array is known for known in arrays):
            arrays.append(array)

    def kernel(where_ref, scale_ref, hidden_ref, other_ref, *refs):
        cots_ref, refs = refs[:2], refs[2:]
        array_refs, refs = refs[: len(arrays)], refs[len(arrays) :]
        if state:
            totals_ref, refs = refs[:2], refs[3:]
        arrived_refs, refs = refs[: (extra + 3) // 4], refs[(extra + 3) // 4 :]
        total_refs, gradient_ref, away_refs, refs = refs[:2], refs[2], refs[3 : 3 + len(chunks)], refs[3 + len(chunks) :]
        hid, cot, wgt, acc, prior, near, far, held, sent, sem, cot_sem, out_sem, near_sem, far_sem = refs
        place = functools.partial(unit_columns, where_ref, rows)
        early = []
        for s in range(2):
            span = pl.ds(s * tokens, tokens)
            source = cots_ref[s].at[pl.ds(0, tokens)]
            early.append(pltpu.make_async_copy(source, cot.at[span], cot_sem.at[s]))
        for copy in early:
            copy.start()
        loads = []
        for b, (array, row, (k, side, part)) in enumerate(units):
            ref = [r for r, known in zip(array_refs, arrays) if known is array][0]
            at = pl.multiple_of((1 - where_ref[2] if part else where_ref[2]) * half, half)
            if len(array.shape) == 3:
                source = ref.at[where_ref[3] ^ k]
            else:
                source = ref.at[pl.ds(at if row is None else row, half)]
            block = (where_ref[3] ^ k) * 2 + (1 - where_ref[1] if side else where_ref[1])
            pairs = [
                (source, wgt.at[b]),
                (hidden_ref.at[:, place((k, side, part), 0)], hid.at[b, pl.ds(0, tokens)]),
                (other_ref.at[block, :, pl.ds(at, half)], hid.at[b, pl.ds(tokens, tokens)]),
            ]
            loads.append([pltpu.make_async_copy(f, t, sem.at[i, b]) for i, (f, t) in enumerate(pairs)])
            for copy in loads[-1]:
                copy.start()
        before = []
        for i, ref in enumerate(arrived_refs):
            size = min(4, extra - 4 * i)
            before.append(pltpu.make_async_copy(ref, held.at[pl.ds(4 * i, size)], cot_sem.at[4 + i]))
        if state:
            for s in range(2):
                span = pl.ds(s * tokens, tokens)
                before.append(pltpu.make_async_copy(totals_ref[s], prior.at[span], cot_sem.at[2 + s]))
        for copy in before:
            copy.start()
        for copy in early:
            copy.wait()
        acc[...] = jnp.zeros_like(acc)

        def step(b, carry):
            for i, ref in enumerate((wgt.at[b], hid.at[b, pl.ds(0, tokens)], hid.at[b, pl.ds(0, tokens)])):
                pltpu.make_async_copy(ref, ref, sem.at[i, b]).wait()
            weight = wgt[b]
            acc[...] += jnp.dot(hid[b], weight, preferred_element_type=F32)
            product = (
                lax.dot_general(
                    cot[...], weight, (((1,), (1,)), ((), ())), preferred_element_type=F32
                )
                * scale_ref[0]
            ).astype(BF16)
            near[b] = product[:tokens]
            far[b] = product[tokens:]
            return carry

        lax.fori_loop(0, count, step, 0)
        late = [
            pltpu.make_async_copy(far.at[pl.ds(4 * i, size)], away_refs[i], far_sem.at[i])
            for i, size in enumerate(chunks)
        ]
        for b, (_, _, unit) in enumerate(units):
            late.append(
                pltpu.make_async_copy(near.at[b], gradient_ref.at[:, place(unit, 0)], near_sem.at[b])
            )
        for copy in late:
            copy.start()
        for copy in before:
            copy.wait()
        if state:
            acc[...] += prior[...]
        sums = [acc.at[pl.ds(s * tokens, tokens)] for s in range(2)]
        if last:
            sent[...] = acc[pl.ds(tokens, tokens)].astype(BF16)
            sums[1] = sent
        end = [pltpu.make_async_copy(sums[s], total_refs[s], out_sem.at[s]) for s in range(2)]
        for e in range(extra):
            columns = place(arrived[1][e], 1)
            end.append(
                pltpu.make_async_copy(held.at[e], gradient_ref.at[:, columns], out_sem.at[2 + e])
            )
        for copy in end:
            copy.start()
        for copy in late + end:
            copy.wait()

    sums = jax.ShapeDtypeStruct((tokens, features), F32)
    operands = [where, scale, hidden, other, *cotangents, *arrays, *state]
    if arrived:
        operands += arrived[0]
    return pl.pallas_call(
        kernel,
        out_shape=[
            sums,
            jax.ShapeDtypeStruct(sums.shape, BF16) if last else sums,
            jax.ShapeDtypeStruct((tokens, width), BF16),
            *[jax.ShapeDtypeStruct((size, tokens, half), BF16) for size in chunks],
        ],
        in_specs=[SMEM, SMEM] + [ANY] * (len(operands) - 2),
        out_specs=[ANY] * (3 + len(chunks)),
        input_output_aliases=(
            {6 + len(arrays) + i: i for i in (0, 2) + (() if last else (1,))} if state else {}
        ),
        scratch_shapes=[
            pltpu.VMEM((count, 2 * tokens, half), BF16),
            pltpu.VMEM((2 * tokens, features), BF16),
            pltpu.VMEM((count, half, features), BF16),
            pltpu.VMEM((2 * tokens, features), F32),
            pltpu.VMEM((2 * tokens, features) if state else (8, 128), F32),
            pltpu.VMEM((count, tokens, half), BF16),
            pltpu.VMEM((count, tokens, half), BF16),
            pltpu.VMEM((max(extra, 1), tokens, half), BF16),
            pltpu.VMEM((tokens, features) if last else (16, 128), BF16),
            pltpu.SemaphoreType.DMA((3, count)),
            pltpu.SemaphoreType.DMA((4 + (extra + 3) // 4,)),
            pltpu.SemaphoreType.DMA((2 + extra,)),
            pltpu.SemaphoreType.DMA((count,)),
            pltpu.SemaphoreType.DMA((len(chunks),)),
        ],
        cost_estimate=CHEAP,
        compiler_params=PARAMS,
        name="consume",
    )(*operands)


def unit_columns(where_ref, rows, unit, core):
    k, side, part = unit
    half = rows // 2
    x = 1 - where_ref[1] if side else where_ref[1]
    c = 1 - where_ref[0] if core else where_ref[0]
    r = 1 - where_ref[2] if part else where_ref[2]
    at = (((where_ref[3] ^ k) * 2 + x) * 2 + c) * rows + r * half
    return pl.ds(pl.multiple_of(at, half), half)


def finish(where, scale, gradient, arrived, units, sums, shares):
    half, features = shares[0].shape
    counts = [len(some) for some in units]

    def kernel(where_ref, scale_ref, *refs):
        arrived_refs, refs = refs[: len(units)], refs[len(units) :]
        a_ref, b_ref, mine_ref, theirs_ref, _, gradient_ref, keys_ref, weight_ref, sem = refs
        copies = []
        for ref, some in zip(arrived_refs, units):
            for e, unit in enumerate(some):
                columns = unit_columns(where_ref, 2 * half, unit, 1)
                copies.append(
                    pltpu.make_async_copy(ref.at[e], gradient_ref.at[:, columns], sem.at[len(copies)])
                )
        for copy in copies:
            copy.start()
        at = pl.multiple_of(where_ref[2] * half, half)
        weight_ref[pl.ds(at, half), :] = mine_ref[...]
        weight_ref[pl.ds(half - at, half), :] = theirs_ref[pl.ds(0, half), :]
        keys_ref[...] = ((a_ref[...] + b_ref[...].astype(F32)) * scale_ref[0]).astype(BF16)
        for copy in copies:
            copy.wait()

    return pl.pallas_call(
        kernel,
        out_shape=[
            jax.ShapeDtypeStruct(gradient.shape, BF16),
            jax.ShapeDtypeStruct(sums[0].shape, BF16),
            jax.ShapeDtypeStruct((2 * half, features), BF16),
        ],
        in_specs=[SMEM, SMEM] + [VMEM] * (len(units) + 4) + [ANY],
        out_specs=[ANY, VMEM, VMEM],
        input_output_aliases={len(units) + 6: 0},
        scratch_shapes=[pltpu.SemaphoreType.DMA((sum(counts),))],
        compiler_params=PARAMS,
        name="finish",
    )(where, scale, *arrived, *sums, *shares, gradient)


def body(hidden, key_weight, previous_peak, cotangent):
    limit = previous_peak[0]
    unscale = limit / 448.0
    scale = unscale.reshape(1)
    tokens = hidden.shape[0]
    rows = key_weight.shape[0]
    r, z, x, c = (lax.axis_index(name) for name in ("replica", "z", "x", "core"))
    where = jnp.stack([c, x, r, z]).astype(jnp.int32)
    nz = lax.axis_size("z")
    token_count = tokens * lax.axis_size(("replica", "z", "x", "core"))

    codes = quantize(key_weight, limit)
    half = rows // 2
    own = lax.dynamic_slice_in_dim(codes, r * half, half, 0)
    rest = lax.dynamic_slice_in_dim(codes, (1 - r) * half, half, 0)
    hidden, own, rest = lax.optimization_barrier((hidden, own, rest))
    mine = lax.all_gather(own, "z", axis=0)
    rest, mine = lax.optimization_barrier((rest, mine))
    theirs = lax.all_gather(rest, "z", axis=0)

    cots = [swap(cotangent, "x"), swap(cotangent, "replica")]
    cut = tokens // 2
    cots += [swap(cots[1][:cut], "x"), swap(cots[0][cut:], "replica")]
    for_group, for_other = pack(where, hidden, rows, nz)
    for_group, *cots = lax.optimization_barrier((for_group, *cots))
    swapped = lax.all_to_all(for_group, ("replica", "x", "core"), 0, 0, tiled=True)
    peaks = jnp.max(jnp.abs(key_weight), axis=0, keepdims=True)
    peaks = jnp.broadcast_to(peaks, (16, peaks.shape[1]))
    for k in (1, 2):
        peaks = jnp.maximum(peaks, swap(peaks, "z", k))
    cots = jnp.concatenate([cotangent, *cots], axis=0)
    cots, peaks = lax.optimization_barrier((cots, peaks))
    cots = [cots, swap(cots, "core")]
    slots = [
        ((r ^ dr) * 2 + (x ^ dx)) * 2 + (c ^ dc) for dc in (0, 1) for dr in (0, 1) for dx in (0, 1)
    ]
    slots = jnp.stack(slots).astype(jnp.int32)
    other = swap(for_other, "core")

    parts = [own] + [lax.dynamic_index_in_dim(mine, z ^ k, keepdims=False) for k in (1, 2, 3)]
    parts[3] = jnp.concatenate([parts[3], peaks])
    swapped, other = lax.optimization_barrier((swapped, other))
    stage = functools.partial(consume, where, scale, hidden, other, [cotangent, cots[1]])

    cots[1], *parts = lax.optimization_barrier((cots[1], *parts))
    side0 = swap(parts[0], "x")
    term = weight_terms(slots, swapped, cots, (0, 1, 2, 3), [])

    term, side0, *parts = lax.optimization_barrier((term, side0, *parts))
    total = lax.psum_scatter(term, "z", scatter_dimension=0, tiled=True).astype(F32)
    side1, other0 = swap(parts[1], "x"), swap(side0, "replica")
    units = [(codes, None, (0, 0, part)) for part in (0, 1)]
    units += [(mine, None, (k, 0, 0)) for k in (1, 2, 3)]
    *state, away0, away1 = stage(units, [], None)
    arrived = ([swap(away0, "core"), swap(away1, "core")], [unit for _, _, unit in units])

    side1, other0, *rest = lax.optimization_barrier((side1, other0, *state, *parts))
    state, parts = rest[:3], rest[3:]
    side2, other1 = swap(parts[2], "x"), swap(side1, "replica")
    units = [(side0, 0, (0, 1, 0)), (other0, 0, (0, 1, 1)), (side1, 0, (1, 1, 0))]
    *state, away = stage(units, state, None)
    late = [swap(away, "core")]
    late_units = [[unit for _, _, unit in units]]

    side2, other1, *rest = lax.optimization_barrier((side2, other1, *state, *parts))
    state, parts = rest[:3], rest[3:]
    side3, other2 = swap(parts[3], "x"), swap(side2, "replica")
    units = [(theirs, None, (k, 0, 1)) for k in (1, 2, 3)]
    *state, away = stage(units, state, arrived)
    arrived = ([swap(away, "core")], [unit for _, _, unit in units])

    side3, other2, *state = lax.optimization_barrier((side3, other2, *state))
    other3 = swap(side3, "replica")
    units = [(other1, 0, (1, 1, 1)), (side2, 0, (2, 1, 0)), (other2, 0, (2, 1, 1)), (side3, 0, (3, 1, 0))]
    *state, away = stage(units, state, arrived)
    late.append(swap(away, "core"))
    late_units.append([unit for _, _, unit in units])

    peak = jnp.maximum(jnp.max(peaks), jnp.max(side3[half:]))
    peak = jnp.full((8, 128), peak.astype(F32))
    peak = jnp.maximum(peak, swap(peak, "core"))
    peak_ratio = (peak[0, 0] / limit).reshape(1)

    share = (total * token_count ** (-0.5)).astype(BF16)
    other_share = swap(jnp.pad(share, ((0, 16), (0, 0))), "replica")
    other3, peak_ratio, *state = lax.optimization_barrier((other3, peak_ratio, *state))
    *state, away = stage([(other3, 0, (3, 1, 1))], state, None, last=True)
    late.append(swap(away, "core"))
    late_units.append([(3, 1, 1)])
    sums = [state[0], swap(state[1], "core")]
    input_gradient, projected_keys, weight_gradient = finish(
        where, scale, state[2], late, late_units, sums, [share, other_share]
    )
    return (projected_keys, input_gradient, weight_gradient, peak_ratio)


def plain(hidden_states, key_weight, previous_peak, key_cotangent):
    names = ("replica", "x", "core")
    limit = previous_peak[0]
    unscale = limit / 448.0
    tokens, width = hidden_states.shape
    rows, features = key_weight.shape
    replicas = lax.axis_size("replica")
    nz, nx, nc = lax.axis_size("z"), lax.axis_size("x"), lax.axis_size("core")
    part = rows // replicas
    group = replicas * nx * nc
    split = hidden_states.reshape(tokens, nz, nx, nc, replicas, part)
    split = split.transpose(4, 2, 3, 0, 1, 5).reshape(group, tokens, nz * part)
    swapped = lax.all_to_all(split, names, 0, 0, tiled=True)
    cotangents = lax.all_gather(key_cotangent, names, axis=0, tiled=True)
    peak = lax.pmax(jnp.max(jnp.abs(key_weight.astype(F32))), ("z", "x", "core"))
    half = lax.dynamic_slice_in_dim(key_weight, lax.axis_index("replica") * part, part, 0)
    gathered = lax.all_gather(
        quantize(half, limit), ("z", "x", "core", "replica"), axis=0, tiled=True
    )
    keys_sum = jnp.dot(hidden_states, gathered, preferred_element_type=F32)
    grad_sum = lax.dot_general(
        key_cotangent, gathered, (((1,), (1,)), ((), ())), preferred_element_type=F32
    )
    term = lax.dot_general(
        swapped.reshape(group * tokens, nz * part),
        cotangents,
        (((0,), (0,)), ((), ())),
        preferred_element_type=F32,
    ).astype(BF16)
    total = lax.psum_scatter(term, "z", scatter_dimension=0, tiled=True).astype(F32)
    token_count = tokens * replicas * nz * nx * nc
    share = (total * token_count ** (-0.5)).astype(BF16)
    weight_gradient = lax.all_gather(share, "replica", axis=0, tiled=True)
    return (
        (keys_sum * unscale).astype(BF16),
        (grad_sum * unscale).astype(BF16),
        weight_gradient,
        (peak / limit).reshape(1),
    )


def solution(mesh):
    replicas, shards = mesh.shape["replica"], mesh.shape["fsdp"]
    grid = Mesh(mesh.devices.reshape(replicas, shards // 4, 2, 2), ("replica", "z", "x", "core"))
    fsdp = ("z", "x", "core")
    every = ("replica",) + fsdp
    in_specs = (P(every, None), P(fsdp, None), P(), P(every, None))
    out_specs = (P(every, None), P(every, None), P(fsdp, None), P())
    run = body if replicas == 2 and shards == 16 else plain
    return jax.shard_map(run, mesh=grid, in_specs=in_specs, out_specs=out_specs, check_vma=False)
```

```python
import functools

import jax
import jax.numpy as jnp
from jax import lax
from jax.experimental import pallas as pl
from jax.experimental.pallas import tpu as pltpu
from jax.sharding import Mesh
from jax.sharding import PartitionSpec as P

ANY = pl.BlockSpec(memory_space=pl.ANY)
SMEM = pl.BlockSpec(memory_space=pltpu.SMEM)
VMEM = pl.BlockSpec(memory_space=pltpu.VMEM)
PARAMS = pltpu.CompilerParams(vmem_limit_bytes=63 * 2**20)
CHEAP = pl.CostEstimate(flops=1, bytes_accessed=1, transcendentals=0)
F32, BF16 = jnp.float32, jnp.bfloat16


def quantize(weight, limit):
    return jnp.clip(weight.astype(F32) * (448.0 / limit), -448.0, 448.0).astype(BF16)


def swap(block, axis, mask=1):
    size = lax.axis_size(axis)
    return lax.ppermute(block, axis, [(i, i ^ mask) for i in range(size)])


def run(copies):
    for copy in copies:
        copy.start()
    for copy in copies:
        copy.wait()


def pack(core, hidden, rows, nz):
    tokens = hidden.shape[0]
    half = rows // 2
    group, blocks = 8, nz * 2

    def kernel(core_ref, hidden_ref, group_ref, other_ref, sem):
        copies = []
        for d in range(group):
            for k in range(nz):
                start = (k * 4 + d % 4) * rows + (d // 4) * half
                copies.append(
                    pltpu.make_async_copy(
                        hidden_ref.at[:, pl.ds(start, half)],
                        group_ref.at[d, :, pl.ds(k * half, half)],
                        sem.at[len(copies)],
                    )
                )
        for b in range(blocks):
            start = pl.multiple_of((b * 2 + 1 - core_ref[0]) * rows, rows)
            copies.append(
                pltpu.make_async_copy(
                    hidden_ref.at[:, pl.ds(start, rows)], other_ref.at[b], sem.at[len(copies)]
                )
            )
        run(copies)

    return pl.pallas_call(
        kernel,
        out_shape=[
            jax.ShapeDtypeStruct((group, tokens, nz * half), BF16),
            jax.ShapeDtypeStruct((blocks, tokens, rows), BF16),
        ],
        in_specs=[SMEM, ANY],
        out_specs=[VMEM, VMEM],
        scratch_shapes=[pltpu.SemaphoreType.DMA((group * nz + blocks,))],
        compiler_params=PARAMS,
        name="pack",
    )(core, hidden)


def weight_terms(slots, swapped, cotangents, tiles, state):
    sources, tokens, width = swapped.shape
    features = cotangents[0].shape[1]
    count = len(tiles)
    tile = width // 4

    def kernel(slots_ref, swapped_ref, *refs):
        cots_ref, refs = refs[:2], refs[2 + len(state) :]
        out_ref, lhs, rhs, out, sem, out_sem = refs
        copies = []
        for s in range(sources):
            place = pl.ds(pl.multiple_of(slots_ref[s] * tokens, tokens), tokens)
            source = cots_ref[s // 4].at[pl.ds(s % 4 * tokens, tokens)]
            copies.append(pltpu.make_async_copy(source, rhs.at[place], sem.at[count, s]))
        for i, t in enumerate(tiles):
            at = pl.ds(t * tile, tile)
            for s in range(sources):
                place = pl.ds(s * tokens, tokens)
                copies.append(
                    pltpu.make_async_copy(swapped_ref.at[s, :, at], lhs.at[i, place], sem.at[i, s])
                )
        for copy in copies:
            copy.start()
        stores = []
        for i, t in enumerate(tiles):
            for copy in copies[(i + 1 if i else 0) * sources : (i + 2) * sources]:
                copy.wait()
            out[i] = lax.dot_general(
                lhs[i], rhs[...], (((0,), (0,)), ((), ())), preferred_element_type=F32
            ).astype(BF16)
            target = out_ref.at[pl.ds(t * tile, tile)]
            stores.append(pltpu.make_async_copy(out.at[i], target, out_sem.at[i]))
            stores[-1].start()
        for copy in stores:
            copy.wait()

    return pl.pallas_call(
        kernel,
        out_shape=jax.ShapeDtypeStruct((width, features), BF16),
        in_specs=[SMEM] + [ANY] * (3 + len(state)),
        out_specs=ANY,
        input_output_aliases={4: 0} if state else {},
        scratch_shapes=[
            pltpu.VMEM((count, sources * tokens, tile), BF16),
            pltpu.VMEM((sources * tokens, features), BF16),
            pltpu.VMEM((count, tile, features), BF16),
            pltpu.SemaphoreType.DMA((count + 1, sources)),
            pltpu.SemaphoreType.DMA((count,)),
        ],
        cost_estimate=CHEAP,
        compiler_params=PARAMS,
        name="weight_terms",
    )(slots, swapped, *cotangents, *state)


def consume(where, scale, hidden, other, cotangents, units, state, arrived, last=False):
    tokens, width = hidden.shape
    rows, features = other.shape[2], cotangents[0].shape[1]
    half = rows // 2
    count = len(units)
    extra = len(arrived[1]) if arrived else 0
    chunks = [min(4, count - i) for i in range(0, count, 4)]
    arrays = []
    for array, _, _ in units:
        if not any(array is known for known in arrays):
            arrays.append(array)

    def kernel(where_ref, scale_ref, hidden_ref, other_ref, *refs):
        cots_ref, refs = refs[:2], refs[2:]
        array_refs, refs = refs[: len(arrays)], refs[len(arrays) :]
        if state:
            totals_ref, refs = refs[:2], refs[3:]
        arrived_refs, refs = refs[: (extra + 3) // 4], refs[(extra + 3) // 4 :]
        total_refs, gradient_ref, away_refs, refs = refs[:2], refs[2], refs[3 : 3 + len(chunks)], refs[3 + len(chunks) :]
        hid, cot, wgt, acc, prior, near, far, held, sent, sem, cot_sem, out_sem, near_sem, far_sem = refs
        place = functools.partial(unit_columns, where_ref, rows)
        early = []
        for s in range(2):
            span = pl.ds(s * tokens, tokens)
            source = cots_ref[s].at[pl.ds(0, tokens)]
            early.append(pltpu.make_async_copy(source, cot.at[span], cot_sem.at[s]))
        for copy in early:
            copy.start()
        loads = []
        for b, (array, row, (k, side, part)) in enumerate(units):
            ref = [r for r, known in zip(array_refs, arrays) if known is array][0]
            at = pl.multiple_of((1 - where_ref[2] if part else where_ref[2]) * half, half)
            if len(array.shape) == 3:
                source = ref.at[where_ref[3] ^ k]
            else:
                source = ref.at[pl.ds(at if row is None else row, half)]
            block = (where_ref[3] ^ k) * 2 + (1 - where_ref[1] if side else where_ref[1])
            pairs = [
                (source, wgt.at[b]),
                (hidden_ref.at[:, place((k, side, part), 0)], hid.at[b, pl.ds(0, tokens)]),
                (other_ref.at[block, :, pl.ds(at, half)], hid.at[b, pl.ds(tokens, tokens)]),
            ]
            loads.append([pltpu.make_async_copy(f, t, sem.at[i, b]) for i, (f, t) in enumerate(pairs)])
            for copy in loads[-1]:
                copy.start()
        before = []
        for i, ref in enumerate(arrived_refs):
            size = min(4, extra - 4 * i)
            before.append(pltpu.make_async_copy(ref, held.at[pl.ds(4 * i, size)], cot_sem.at[4 + i]))
        if state:
            for s in range(2):
                span = pl.ds(s * tokens, tokens)
                before.append(pltpu.make_async_copy(totals_ref[s], prior.at[span], cot_sem.at[2 + s]))
        for copy in before:
            copy.start()
        for copy in early:
            copy.wait()
        acc[...] = jnp.zeros_like(acc)

        def step(b, carry):
            for i, ref in enumerate((wgt.at[b], hid.at[b, pl.ds(0, tokens)], hid.at[b, pl.ds(0, tokens)])):
                pltpu.make_async_copy(ref, ref, sem.at[i, b]).wait()
            weight = wgt[b]
            acc[...] += jnp.dot(hid[b], weight, preferred_element_type=F32)
            product = (
                lax.dot_general(
                    cot[...], weight, (((1,), (1,)), ((), ())), preferred_element_type=F32
                )
                * scale_ref[0]
            ).astype(BF16)
            near[b] = product[:tokens]
            far[b] = product[tokens:]
            return carry

        lax.fori_loop(0, count, step, 0)
        late = [
            pltpu.make_async_copy(far.at[pl.ds(4 * i, size)], away_refs[i], far_sem.at[i])
            for i, size in enumerate(chunks)
        ]
        for b, (_, _, unit) in enumerate(units):
            late.append(
                pltpu.make_async_copy(near.at[b], gradient_ref.at[:, place(unit, 0)], near_sem.at[b])
            )
        for copy in late:
            copy.start()
        for copy in before:
            copy.wait()
        if state:
            acc[...] += prior[...]
        sums = [acc.at[pl.ds(s * tokens, tokens)] for s in range(2)]
        if last:
            sent[...] = acc[pl.ds(tokens, tokens)].astype(BF16)
            sums[1] = sent
        end = [pltpu.make_async_copy(sums[s], total_refs[s], out_sem.at[s]) for s in range(2)]
        for e in range(extra):
            columns = place(arrived[1][e], 1)
            end.append(
                pltpu.make_async_copy(held.at[e], gradient_ref.at[:, columns], out_sem.at[2 + e])
            )
        for copy in end:
            copy.start()
        for copy in late + end:
            copy.wait()

    sums = jax.ShapeDtypeStruct((tokens, features), F32)
    operands = [where, scale, hidden, other, *cotangents, *arrays, *state]
    if arrived:
        operands += arrived[0]
    return pl.pallas_call(
        kernel,
        out_shape=[
            sums,
            jax.ShapeDtypeStruct(sums.shape, BF16) if last else sums,
            jax.ShapeDtypeStruct((tokens, width), BF16),
            *[jax.ShapeDtypeStruct((size, tokens, half), BF16) for size in chunks],
        ],
        in_specs=[SMEM, SMEM] + [ANY] * (len(operands) - 2),
        out_specs=[ANY] * (3 + len(chunks)),
        input_output_aliases=(
            {6 + len(arrays) + i: i for i in (0, 2) + (() if last else (1,))} if state else {}
        ),
        scratch_shapes=[
            pltpu.VMEM((count, 2 * tokens, half), BF16),
            pltpu.VMEM((2 * tokens, features), BF16),
            pltpu.VMEM((count, half, features), BF16),
            pltpu.VMEM((2 * tokens, features), F32),
            pltpu.VMEM((2 * tokens, features) if state else (8, 128), F32),
            pltpu.VMEM((count, tokens, half), BF16),
            pltpu.VMEM((count, tokens, half), BF16),
            pltpu.VMEM((max(extra, 1), tokens, half), BF16),
            pltpu.VMEM((tokens, features) if last else (16, 128), BF16),
            pltpu.SemaphoreType.DMA((3, count)),
            pltpu.SemaphoreType.DMA((4 + (extra + 3) // 4,)),
            pltpu.SemaphoreType.DMA((2 + extra,)),
            pltpu.SemaphoreType.DMA((count,)),
            pltpu.SemaphoreType.DMA((len(chunks),)),
        ],
        cost_estimate=CHEAP,
        compiler_params=PARAMS,
        name="consume",
    )(*operands)


def unit_columns(where_ref, rows, unit, core):
    k, side, part = unit
    half = rows // 2
    x = 1 - where_ref[1] if side else where_ref[1]
    c = 1 - where_ref[0] if core else where_ref[0]
    r = 1 - where_ref[2] if part else where_ref[2]
    at = (((where_ref[3] ^ k) * 2 + x) * 2 + c) * rows + r * half
    return pl.ds(pl.multiple_of(at, half), half)


def finish(where, scale, gradient, arrived, units, sums):
    half = arrived[0].shape[2]
    counts = [len(some) for some in units]

    def kernel(where_ref, scale_ref, *refs):
        arrived_refs, refs = refs[: len(units)], refs[len(units) :]
        a_ref, b_ref, _, gradient_ref, keys_ref, sem = refs
        copies = []
        for ref, some in zip(arrived_refs, units):
            for e, unit in enumerate(some):
                columns = unit_columns(where_ref, 2 * half, unit, 1)
                copies.append(
                    pltpu.make_async_copy(ref.at[e], gradient_ref.at[:, columns], sem.at[len(copies)])
                )
        for copy in copies:
            copy.start()
        keys_ref[...] = ((a_ref[...] + b_ref[...].astype(F32)) * scale_ref[0]).astype(BF16)
        for copy in copies:
            copy.wait()

    return pl.pallas_call(
        kernel,
        out_shape=[
            jax.ShapeDtypeStruct(gradient.shape, BF16),
            jax.ShapeDtypeStruct(sums[0].shape, BF16),
        ],
        in_specs=[SMEM, SMEM] + [VMEM] * (len(units) + 2) + [ANY],
        out_specs=[ANY, VMEM],
        input_output_aliases={len(units) + 4: 0},
        scratch_shapes=[pltpu.SemaphoreType.DMA((sum(counts),))],
        compiler_params=PARAMS,
        name="finish",
    )(where, scale, *arrived, *sums, gradient)


def join(where, mine, theirs):
    half, features = mine.shape

    def kernel(where_ref, mine_ref, theirs_ref, out_ref):
        at = pl.multiple_of(where_ref[2] * half, half)
        out_ref[pl.ds(at, half), :] = mine_ref[...]
        out_ref[pl.ds(half - at, half), :] = theirs_ref[pl.ds(0, half), :]

    return pl.pallas_call(
        kernel,
        out_shape=jax.ShapeDtypeStruct((2 * half, features), BF16),
        in_specs=[SMEM, VMEM, VMEM],
        out_specs=VMEM,
        compiler_params=PARAMS,
        name="join",
    )(where, mine, theirs)


def body(hidden, key_weight, previous_peak, cotangent):
    limit = previous_peak[0]
    unscale = limit / 448.0
    scale = unscale.reshape(1)
    tokens = hidden.shape[0]
    rows = key_weight.shape[0]
    r, z, x, c = (lax.axis_index(name) for name in ("replica", "z", "x", "core"))
    where = jnp.stack([c, x, r, z]).astype(jnp.int32)
    nz = lax.axis_size("z")
    token_count = tokens * lax.axis_size(("replica", "z", "x", "core"))

    codes = quantize(key_weight, limit)
    half = rows // 2
    own = lax.dynamic_slice_in_dim(codes, r * half, half, 0)
    rest = lax.dynamic_slice_in_dim(codes, (1 - r) * half, half, 0)
    hidden, own, rest = lax.optimization_barrier((hidden, own, rest))
    mine = lax.all_gather(own, "z", axis=0)
    rest, mine = lax.optimization_barrier((rest, mine))
    theirs = lax.all_gather(rest, "z", axis=0)

    cots = [swap(cotangent, "x"), swap(cotangent, "replica")]
    for_group, for_other = pack(where, hidden, rows, nz)
    for_group, *cots = lax.optimization_barrier((for_group, *cots))
    cut = tokens // 2
    cots += [swap(cots[1][:cut], "x"), swap(cots[0][cut:], "replica")]
    for_group, *cots = lax.optimization_barrier((for_group, *cots))
    swapped = lax.all_to_all(for_group, ("replica", "x", "core"), 0, 0, tiled=True)
    peaks = jnp.max(jnp.abs(key_weight), axis=0, keepdims=True)
    peaks = jnp.broadcast_to(peaks, (16, peaks.shape[1]))
    for k in (1, 2):
        peaks = jnp.maximum(peaks, swap(peaks, "z", k))
    cots = jnp.concatenate([cotangent, *cots], axis=0)
    cots, peaks = lax.optimization_barrier((cots, peaks))
    cots = [cots, swap(cots, "core")]
    slots = [
        ((r ^ dr) * 2 + (x ^ dx)) * 2 + (c ^ dc) for dc in (0, 1) for dr in (0, 1) for dx in (0, 1)
    ]
    slots = jnp.stack(slots).astype(jnp.int32)
    other = swap(for_other, "core")

    parts = [jnp.concatenate([own, peaks])]
    parts += [lax.dynamic_index_in_dim(mine, z ^ k, keepdims=False) for k in (1, 2, 3)]
    cots[1], *parts = lax.optimization_barrier((cots[1], *parts))
    side0 = swap(parts[0], "x")
    swapped, other = lax.optimization_barrier((swapped, other))
    term = weight_terms(slots, swapped, cots, (0, 1, 2, 3), [])
    stage = functools.partial(consume, where, scale, hidden, other, [cotangent, cots[1]])

    def codes_of(units):
        return [unit for _, _, unit in units]

    term, side0, *parts = lax.optimization_barrier((term, side0, *parts))
    total = lax.psum_scatter(term, "z", scatter_dimension=0, tiled=True).astype(F32)
    side1, other0 = swap(parts[1], "x"), swap(side0[:half], "replica")
    units = [(codes, None, (0, 0, part)) for part in (0, 1)] + [(mine, None, (k, 0, 0)) for k in (1, 2, 3)]
    *state, away0, away1 = stage(units, [], None)
    first = ([swap(away0, "core"), swap(away1, "core")], codes_of(units))

    side1, other0, *rest = lax.optimization_barrier((side1, other0, *state, *parts))
    state, parts = rest[:3], rest[3:]
    side2, other1 = swap(parts[2], "x"), swap(side1, "replica")
    units = [(side0, 0, (0, 1, 0)), (other0, 0, (0, 1, 1)), (side1, 0, (1, 1, 0)), (theirs, None, (1, 0, 1))]
    *state, away = stage(units, state, None)
    second = ([swap(away, "core")], codes_of(units))

    side2, other1, *rest = lax.optimization_barrier((side2, other1, *state, *parts))
    state, parts = rest[:3], rest[3:]
    side3, other2 = swap(parts[3], "x"), swap(side2, "replica")
    units = [(theirs, None, (2, 0, 1)), (theirs, None, (3, 0, 1)), (other1, 0, (1, 1, 1)), (side2, 0, (2, 1, 0))]
    *state, away = stage(units, state, first)
    late, late_units = [swap(away, "core")], [codes_of(units)]

    rest = lax.dynamic_index_in_dim(theirs, z ^ 3, keepdims=False)
    side3, other2, rest, *state = lax.optimization_barrier((side3, other2, rest, *state))
    other3 = swap(rest, "x")
    units = [(other2, 0, (2, 1, 1)), (side3, 0, (3, 1, 0))]
    *state, away = stage(units, state, second)
    late.append(swap(away, "core"))
    late_units.append(codes_of(units))

    peak = jnp.maximum(jnp.max(peaks), jnp.max(side0[half:]))
    peak = jnp.full((8, 128), peak.astype(F32))
    peak = jnp.maximum(peak, swap(peak, "core"))
    peak_ratio = (peak[0, 0] / limit).reshape(1)

    share = (total * token_count ** (-0.5)).astype(BF16)
    other_share = swap(jnp.pad(share, ((0, 16), (0, 0))), "replica")
    other3, peak_ratio, *state = lax.optimization_barrier((other3, peak_ratio, *state))
    *state, away = stage([(other3, 0, (3, 1, 1))], state, None, last=True)
    late.append(swap(away, "core"))
    late_units.append([(3, 1, 1)])
    sums = [state[0], swap(state[1], "core")]
    input_gradient, projected_keys = finish(where, scale, state[2], late, late_units, sums)
    weight_gradient = join(where, share, other_share)
    return (projected_keys, input_gradient, weight_gradient, peak_ratio)


def plain(hidden_states, key_weight, previous_peak, key_cotangent):
    names = ("replica", "x", "core")
    limit = previous_peak[0]
    unscale = limit / 448.0
    tokens, width = hidden_states.shape
    rows, features = key_weight.shape
    replicas = lax.axis_size("replica")
    nz, nx, nc = lax.axis_size("z"), lax.axis_size("x"), lax.axis_size("core")
    part = rows // replicas
    group = replicas * nx * nc
    split = hidden_states.reshape(tokens, nz, nx, nc, replicas, part)
    split = split.transpose(4, 2, 3, 0, 1, 5).reshape(group, tokens, nz * part)
    swapped = lax.all_to_all(split, names, 0, 0, tiled=True)
    cotangents = lax.all_gather(key_cotangent, names, axis=0, tiled=True)
    peak = lax.pmax(jnp.max(jnp.abs(key_weight.astype(F32))), ("z", "x", "core"))
    half = lax.dynamic_slice_in_dim(key_weight, lax.axis_index("replica") * part, part, 0)
    gathered = lax.all_gather(
        quantize(half, limit), ("z", "x", "core", "replica"), axis=0, tiled=True
    )
    keys_sum = jnp.dot(hidden_states, gathered, preferred_element_type=F32)
    grad_sum = lax.dot_general(
        key_cotangent, gathered, (((1,), (1,)), ((), ())), preferred_element_type=F32
    )
    term = lax.dot_general(
        swapped.reshape(group * tokens, nz * part),
        cotangents,
        (((0,), (0,)), ((), ())),
        preferred_element_type=F32,
    ).astype(BF16)
    total = lax.psum_scatter(term, "z", scatter_dimension=0, tiled=True).astype(F32)
    token_count = tokens * replicas * nz * nx * nc
    share = (total * token_count ** (-0.5)).astype(BF16)
    weight_gradient = lax.all_gather(share, "replica", axis=0, tiled=True)
    return (
        (keys_sum * unscale).astype(BF16),
        (grad_sum * unscale).astype(BF16),
        weight_gradient,
        (peak / limit).reshape(1),
    )


def solution(mesh):
    replicas, shards = mesh.shape["replica"], mesh.shape["fsdp"]
    grid = Mesh(mesh.devices.reshape(replicas, shards // 4, 2, 2), ("replica", "z", "x", "core"))
    fsdp = ("z", "x", "core")
    every = ("replica",) + fsdp
    in_specs = (P(every, None), P(fsdp, None), P(), P(every, None))
    out_specs = (P(every, None), P(every, None), P(fsdp, None), P())
    run = body if replicas == 2 and shards == 16 else plain
    return jax.shard_map(run, mesh=grid, in_specs=in_specs, out_specs=out_specs, check_vma=False)
```

```python
import functools

import jax
import jax.numpy as jnp
from jax import lax
from jax.experimental import pallas as pl
from jax.experimental.pallas import tpu as pltpu
from jax.sharding import Mesh
from jax.sharding import PartitionSpec as P

ANY = pl.BlockSpec(memory_space=pl.ANY)
SMEM = pl.BlockSpec(memory_space=pltpu.SMEM)
VMEM = pl.BlockSpec(memory_space=pltpu.VMEM)
PARAMS = pltpu.CompilerParams(vmem_limit_bytes=63 * 2**20)
CHEAP = pl.CostEstimate(flops=1, bytes_accessed=1, transcendentals=0)
F32, BF16 = jnp.float32, jnp.bfloat16


def quantize(weight, limit):
    return jnp.clip(weight.astype(F32) * (448.0 / limit), -448.0, 448.0).astype(BF16)


def swap(block, axis, mask=1):
    size = lax.axis_size(axis)
    return lax.ppermute(block, axis, [(i, i ^ mask) for i in range(size)])


def run(copies):
    for copy in copies:
        copy.start()
    for copy in copies:
        copy.wait()


def pack(core, hidden, rows, nz):
    tokens = hidden.shape[0]
    half = rows // 2
    group, blocks = 8, nz * 2

    def kernel(core_ref, hidden_ref, group_ref, other_ref, sem):
        copies = []
        for d in range(group):
            for k in range(nz):
                start = (k * 4 + d % 4) * rows + (d // 4) * half
                copies.append(
                    pltpu.make_async_copy(
                        hidden_ref.at[:, pl.ds(start, half)],
                        group_ref.at[d, :, pl.ds(k * half, half)],
                        sem.at[len(copies)],
                    )
                )
        for b in range(blocks):
            start = pl.multiple_of((b * 2 + 1 - core_ref[0]) * rows, rows)
            copies.append(
                pltpu.make_async_copy(
                    hidden_ref.at[:, pl.ds(start, rows)], other_ref.at[b], sem.at[len(copies)]
                )
            )
        run(copies)

    return pl.pallas_call(
        kernel,
        out_shape=[
            jax.ShapeDtypeStruct((group, tokens, nz * half), BF16),
            jax.ShapeDtypeStruct((blocks, tokens, rows), BF16),
        ],
        in_specs=[SMEM, ANY],
        out_specs=[VMEM, VMEM],
        scratch_shapes=[pltpu.SemaphoreType.DMA((group * nz + blocks,))],
        compiler_params=PARAMS,
        name="pack",
    )(core, hidden)


def weight_terms(slots, swapped, cotangents, tiles, state):
    sources, tokens, width = swapped.shape
    features = cotangents[0].shape[1]
    count = len(tiles)
    tile = width // 4

    def kernel(slots_ref, swapped_ref, *refs):
        cots_ref, refs = refs[:4], refs[4 + len(state) :]
        out_ref, lhs, rhs, out, sem, out_sem = refs
        copies = []
        for s in range(sources):
            place = pl.ds(pl.multiple_of(slots_ref[s] * tokens, tokens), tokens)
            source = cots_ref[s // 4].at[pl.ds(s % 4 * tokens, tokens)] if s % 4 < 3 else cots_ref[2 + s // 4]
            copies.append(pltpu.make_async_copy(source, rhs.at[place], sem.at[count, s]))
        for i, t in enumerate(tiles):
            at = pl.ds(t * tile, tile)
            for s in range(sources):
                place = pl.ds(s * tokens, tokens)
                copies.append(
                    pltpu.make_async_copy(swapped_ref.at[s, :, at], lhs.at[i, place], sem.at[i, s])
                )
        for copy in copies:
            copy.start()
        stores = []
        for i, t in enumerate(tiles):
            for copy in copies[(i + 1 if i else 0) * sources : (i + 2) * sources]:
                copy.wait()
            out[i] = lax.dot_general(
                lhs[i], rhs[...], (((0,), (0,)), ((), ())), preferred_element_type=F32
            ).astype(BF16)
            target = out_ref.at[pl.ds(t * tile, tile)]
            stores.append(pltpu.make_async_copy(out.at[i], target, out_sem.at[i]))
            stores[-1].start()
        for copy in stores:
            copy.wait()

    return pl.pallas_call(
        kernel,
        out_shape=jax.ShapeDtypeStruct((width, features), BF16),
        in_specs=[SMEM] + [ANY] * (5 + len(state)),
        out_specs=ANY,
        input_output_aliases={6: 0} if state else {},
        scratch_shapes=[
            pltpu.VMEM((count, sources * tokens, tile), BF16),
            pltpu.VMEM((sources * tokens, features), BF16),
            pltpu.VMEM((count, tile, features), BF16),
            pltpu.SemaphoreType.DMA((count + 1, sources)),
            pltpu.SemaphoreType.DMA((count,)),
        ],
        cost_estimate=CHEAP,
        compiler_params=PARAMS,
        name="weight_terms",
    )(slots, swapped, *cotangents, *state)


def consume(where, scale, hidden, other, cotangents, units, state, arrived, last=False):
    tokens, width = hidden.shape
    rows, features = other.shape[2], cotangents[0].shape[1]
    half = rows // 2
    count = len(units)
    extra = len(arrived[1]) if arrived else 0
    chunks = [min(4, count - i) for i in range(0, count, 4)]
    arrays = []
    for array, _, _ in units:
        if not any(array is known for known in arrays):
            arrays.append(array)

    def kernel(where_ref, scale_ref, hidden_ref, other_ref, *refs):
        cots_ref, refs = refs[:2], refs[2:]
        array_refs, refs = refs[: len(arrays)], refs[len(arrays) :]
        if state:
            totals_ref, refs = refs[:2], refs[3:]
        arrived_refs, refs = refs[: (extra + 3) // 4], refs[(extra + 3) // 4 :]
        total_refs, gradient_ref, away_refs, refs = refs[:2], refs[2], refs[3 : 3 + len(chunks)], refs[3 + len(chunks) :]
        hid, cot, wgt, acc, prior, near, far, held, sent, sem, cot_sem, out_sem, near_sem, far_sem = refs
        place = functools.partial(unit_columns, where_ref, rows)
        early = []
        for s in range(2):
            span = pl.ds(s * tokens, tokens)
            source = cots_ref[s].at[pl.ds(0, tokens)]
            early.append(pltpu.make_async_copy(source, cot.at[span], cot_sem.at[s]))
        for copy in early:
            copy.start()
        loads = []
        for b, (array, row, (k, side, part)) in enumerate(units):
            ref = [r for r, known in zip(array_refs, arrays) if known is array][0]
            at = pl.multiple_of((1 - where_ref[2] if part else where_ref[2]) * half, half)
            source = ref.at[where_ref[3] ^ k] if row is None else ref.at[pl.ds(row, half)]
            block = (where_ref[3] ^ k) * 2 + (1 - where_ref[1] if side else where_ref[1])
            pairs = [
                (source, wgt.at[b]),
                (hidden_ref.at[:, place((k, side, part), 0)], hid.at[b, pl.ds(0, tokens)]),
                (other_ref.at[block, :, pl.ds(at, half)], hid.at[b, pl.ds(tokens, tokens)]),
            ]
            loads.append([pltpu.make_async_copy(f, t, sem.at[i, b]) for i, (f, t) in enumerate(pairs)])
            for copy in loads[-1]:
                copy.start()
        before = []
        for i, ref in enumerate(arrived_refs):
            size = min(4, extra - 4 * i)
            before.append(pltpu.make_async_copy(ref, held.at[pl.ds(4 * i, size)], cot_sem.at[4 + i]))
        if state:
            for s in range(2):
                span = pl.ds(s * tokens, tokens)
                before.append(pltpu.make_async_copy(totals_ref[s], prior.at[span], cot_sem.at[2 + s]))
        for copy in before:
            copy.start()
        for copy in early:
            copy.wait()
        acc[...] = jnp.zeros_like(acc)

        def step(b, carry):
            for i, ref in enumerate((wgt.at[b], hid.at[b, pl.ds(0, tokens)], hid.at[b, pl.ds(0, tokens)])):
                pltpu.make_async_copy(ref, ref, sem.at[i, b]).wait()
            weight = wgt[b]
            acc[...] += jnp.dot(hid[b], weight, preferred_element_type=F32)
            product = (
                lax.dot_general(
                    cot[...], weight, (((1,), (1,)), ((), ())), preferred_element_type=F32
                )
                * scale_ref[0]
            ).astype(BF16)
            near[b] = product[:tokens]
            far[b] = product[tokens:]
            return carry

        lax.fori_loop(0, count, step, 0)
        late = [
            pltpu.make_async_copy(far.at[pl.ds(4 * i, size)], away_refs[i], far_sem.at[i])
            for i, size in enumerate(chunks)
        ]
        for b, (_, _, unit) in enumerate(units):
            late.append(
                pltpu.make_async_copy(near.at[b], gradient_ref.at[:, place(unit, 0)], near_sem.at[b])
            )
        for copy in late:
            copy.start()
        for copy in before:
            copy.wait()
        if state:
            acc[...] += prior[...]
        sums = [acc.at[pl.ds(s * tokens, tokens)] for s in range(2)]
        if last:
            sent[...] = acc[pl.ds(tokens, tokens)].astype(BF16)
            sums[1] = sent
        end = [pltpu.make_async_copy(sums[s], total_refs[s], out_sem.at[s]) for s in range(2)]
        for e in range(extra):
            columns = place(arrived[1][e], 1)
            end.append(
                pltpu.make_async_copy(held.at[e], gradient_ref.at[:, columns], out_sem.at[2 + e])
            )
        for copy in end:
            copy.start()
        for copy in late + end:
            copy.wait()

    sums = jax.ShapeDtypeStruct((tokens, features), F32)
    operands = [where, scale, hidden, other, *cotangents, *arrays, *state]
    if arrived:
        operands += arrived[0]
    return pl.pallas_call(
        kernel,
        out_shape=[
            sums,
            jax.ShapeDtypeStruct(sums.shape, BF16) if last else sums,
            jax.ShapeDtypeStruct((tokens, width), BF16),
            *[jax.ShapeDtypeStruct((size, tokens, half), BF16) for size in chunks],
        ],
        in_specs=[SMEM, SMEM] + [ANY] * (len(operands) - 2),
        out_specs=[ANY] * (3 + len(chunks)),
        input_output_aliases=(
            {6 + len(arrays) + i: i for i in (0, 2) + (() if last else (1,))} if state else {}
        ),
        scratch_shapes=[
            pltpu.VMEM((count, 2 * tokens, half), BF16),
            pltpu.VMEM((2 * tokens, features), BF16),
            pltpu.VMEM((count, half, features), BF16),
            pltpu.VMEM((2 * tokens, features), F32),
            pltpu.VMEM((2 * tokens, features) if state else (8, 128), F32),
            pltpu.VMEM((count, tokens, half), BF16),
            pltpu.VMEM((count, tokens, half), BF16),
            pltpu.VMEM((max(extra, 1), tokens, half), BF16),
            pltpu.VMEM((tokens, features) if last else (16, 128), BF16),
            pltpu.SemaphoreType.DMA((3, count)),
            pltpu.SemaphoreType.DMA((4 + (extra + 3) // 4,)),
            pltpu.SemaphoreType.DMA((2 + extra,)),
            pltpu.SemaphoreType.DMA((count,)),
            pltpu.SemaphoreType.DMA((len(chunks),)),
        ],
        cost_estimate=CHEAP,
        compiler_params=PARAMS,
        name="consume",
    )(*operands)


def unit_columns(where_ref, rows, unit, core):
    k, side, part = unit
    half = rows // 2
    x = 1 - where_ref[1] if side else where_ref[1]
    c = 1 - where_ref[0] if core else where_ref[0]
    r = 1 - where_ref[2] if part else where_ref[2]
    at = (((where_ref[3] ^ k) * 2 + x) * 2 + c) * rows + r * half
    return pl.ds(pl.multiple_of(at, half), half)


def finish(where, scale, hidden, cotangent, unit, weights, sums, gradient, arrived, units):
    tokens, width = hidden.shape
    half, features = weights[0].shape
    counts = [len(some) for some in units]

    def kernel(where_ref, scale_ref, hidden_ref, cot_ref, *refs):
        weight_refs, sum_refs, arrived_refs, refs = refs[:2], refs[2:4], refs[4 : 4 + len(units)], refs[5 + len(units) :]
        gradient_ref, keys_ref, hid, cot, wgt, near, far, held, new, sem, held_sem, out_sem = refs
        place = functools.partial(unit_columns, where_ref, 2 * half)
        loads = [pltpu.make_async_copy(cot_ref, cot, sem.at[0])]
        for i in range(2):
            loads.append(pltpu.make_async_copy(weight_refs[i], wgt.at[i], sem.at[1 + i]))
            columns = hidden_ref.at[:, place(unit, i)]
            loads.append(pltpu.make_async_copy(columns, hid.at[i], sem.at[3 + i]))
        loads.append(pltpu.make_async_copy(sum_refs[0], near, sem.at[5]))
        loads.append(pltpu.make_async_copy(sum_refs[1], far, sem.at[6]))
        for copy in loads:
            copy.start()
        fills, stores = [], []
        for j, (ref, some) in enumerate(zip(arrived_refs, units)):
            first = sum(counts[:j])
            fills.append(pltpu.make_async_copy(ref, held.at[pl.ds(first, len(some))], held_sem.at[j]))
            fills[-1].start()
            for e, one in enumerate(some):
                target = gradient_ref.at[:, place(one, 1)]
                stores.append(pltpu.make_async_copy(held.at[first + e], target, out_sem.at[2 + first + e]))
        for copy in loads[:5]:
            copy.wait()
        for i in range(2):
            new[i] = (
                lax.dot_general(
                    cot[...], wgt[i], (((1,), (1,)), ((), ())), preferred_element_type=F32
                )
                * scale_ref[0]
            ).astype(BF16)
            target = gradient_ref.at[:, place(unit, i)]
            stores.append(pltpu.make_async_copy(new.at[i], target, out_sem.at[i]))
            stores[-1].start()
        for copy in fills:
            copy.wait()
        for copy in stores[:-2]:
            copy.start()
        total = jnp.dot(hid[0], wgt[0], preferred_element_type=F32)
        total += jnp.dot(hid[1], wgt[1], preferred_element_type=F32)
        for copy in loads[5:]:
            copy.wait()
        keys_ref[...] = ((total + near[...] + far[...].astype(F32)) * scale_ref[0]).astype(BF16)
        for copy in stores:
            copy.wait()

    return pl.pallas_call(
        kernel,
        out_shape=[
            jax.ShapeDtypeStruct(gradient.shape, BF16),
            jax.ShapeDtypeStruct((tokens, features), BF16),
        ],
        in_specs=[SMEM, SMEM] + [ANY] * (7 + len(units)),
        out_specs=[ANY, VMEM],
        input_output_aliases={8 + len(units): 0},
        scratch_shapes=[
            pltpu.VMEM((2, tokens, half), BF16),
            pltpu.VMEM((tokens, features), BF16),
            pltpu.VMEM((2, half, features), BF16),
            pltpu.VMEM((tokens, features), F32),
            pltpu.VMEM((tokens, features), BF16),
            pltpu.VMEM((sum(counts), tokens, half), BF16),
            pltpu.VMEM((2, tokens, half), BF16),
            pltpu.SemaphoreType.DMA((7,)),
            pltpu.SemaphoreType.DMA((len(units),)),
            pltpu.SemaphoreType.DMA((2 + sum(counts),)),
        ],
        cost_estimate=CHEAP,
        compiler_params=PARAMS,
        name="finish",
    )(where, scale, hidden, cotangent, *weights, *sums, *arrived, gradient)


def join(where, mine, theirs):
    half, features = mine.shape

    def kernel(where_ref, mine_ref, theirs_ref, out_ref):
        at = pl.multiple_of(where_ref[2] * half, half)
        out_ref[pl.ds(at, half), :] = mine_ref[...]
        out_ref[pl.ds(half - at, half), :] = theirs_ref[pl.ds(0, half), :]

    return pl.pallas_call(
        kernel,
        out_shape=jax.ShapeDtypeStruct((2 * half, features), BF16),
        in_specs=[SMEM, VMEM, VMEM],
        out_specs=VMEM,
        compiler_params=PARAMS,
        name="join",
    )(where, mine, theirs)


def body(hidden, key_weight, previous_peak, cotangent):
    limit = previous_peak[0]
    unscale = limit / 448.0
    scale = unscale.reshape(1)
    tokens = hidden.shape[0]
    rows = key_weight.shape[0]
    r, z, x, c = (lax.axis_index(name) for name in ("replica", "z", "x", "core"))
    where = jnp.stack([c, x, r, z]).astype(jnp.int32)
    nz = lax.axis_size("z")
    token_count = tokens * lax.axis_size(("replica", "z", "x", "core"))

    half = rows // 2
    own = quantize(lax.dynamic_slice_in_dim(key_weight, r * half, half, 0), limit)
    rest = quantize(lax.dynamic_slice_in_dim(key_weight, (1 - r) * half, half, 0), limit)
    hidden, own, rest = lax.optimization_barrier((hidden, own, rest))
    mine = lax.all_gather(own, "z", axis=0)
    rest0, mine = lax.optimization_barrier((rest, mine))
    rest1, rest2 = swap(rest0, "z", 1), swap(rest0, "z", 2)

    cots = [swap(cotangent, "x"), swap(cotangent, "replica")]
    for_group, for_other = pack(where, hidden, rows, nz)
    for_group, *cots = lax.optimization_barrier((for_group, *cots))
    swapped = lax.all_to_all(for_group, ("replica", "x", "core"), 0, 0, tiled=True)
    cut = tokens // 2
    diagonal = [swap(cots[1][:cut], "x"), swap(cots[0][cut:], "replica")]
    peaks = jnp.max(jnp.abs(key_weight), axis=0, keepdims=True)
    peaks = jnp.broadcast_to(peaks, (16, peaks.shape[1]))
    for k in (1, 2):
        peaks = jnp.maximum(peaks, swap(peaks, "z", k))
    cots = jnp.concatenate([cotangent, *cots], axis=0)
    cots, peaks = lax.optimization_barrier((cots, peaks))
    cots = [cots, swap(cots, "core")]
    rest1, rest2, *diagonal = lax.optimization_barrier((rest1, rest2, *diagonal))
    diagonal = jnp.concatenate(diagonal, axis=0)
    diagonal = [diagonal, swap(diagonal, "core")]
    slots = [
        ((r ^ dr) * 2 + (x ^ dx)) * 2 + (c ^ dc) for dc in (0, 1) for dr in (0, 1) for dx in (0, 1)
    ]
    slots = jnp.stack(slots).astype(jnp.int32)
    other = swap(for_other, "core")

    parts = [jnp.concatenate([own, peaks])]
    parts += [lax.dynamic_index_in_dim(mine, z ^ k, keepdims=False) for k in (1, 2, 3)]
    cots[1], *parts = lax.optimization_barrier((cots[1], *parts))
    side0, rest3 = swap(parts[0], "x"), swap(parts[3], "replica")
    swapped, other = lax.optimization_barrier((swapped, other))
    term = weight_terms(slots, swapped, cots + diagonal, (0, 1, 2, 3), [])
    stage = functools.partial(consume, where, scale, hidden, other, [cotangent, cots[1]])

    def codes_of(units):
        return [unit for _, _, unit in units]

    term, side0, rest3, *parts = lax.optimization_barrier((term, side0, rest3, *parts))
    total = lax.psum_scatter(term, "z", scatter_dimension=0, tiled=True)
    side1, other0 = swap(parts[1], "x"), swap(side0[:half], "replica")
    units = [(own, 0, (0, 0, 0)), (rest0, 0, (0, 0, 1))] + [(mine, None, (k, 0, 0)) for k in (1, 2, 3)]
    *state, away0, away1 = stage(units, [], None)
    first = ([swap(away0, "core"), swap(away1, "core")], codes_of(units))

    side1, other0, *rest = lax.optimization_barrier((side1, other0, *state, *parts))
    state, parts = rest[:3], rest[3:]
    side2, other1 = swap(parts[2], "x"), swap(side1, "replica")
    units = [(side0, 0, (0, 1, 0)), (other0, 0, (0, 1, 1)), (side1, 0, (1, 1, 0)), (rest1, 0, (1, 0, 1))]
    *state, away = stage(units, state, None)
    second = ([swap(away, "core")], codes_of(units))

    side2, other1, *rest = lax.optimization_barrier((side2, other1, *state, *parts))
    state, parts = rest[:3], rest[3:]
    side3, other2 = swap(parts[3], "x"), swap(side2, "replica")
    units = [(rest2, 0, (2, 0, 1)), (rest3, 0, (3, 0, 1)), (other1, 0, (1, 1, 1)), (side2, 0, (2, 1, 0))]
    *state, away = stage(units, state, first)
    late, late_units = [swap(away, "core")], [codes_of(units)]

    side3, other2, rest3, *state = lax.optimization_barrier((side3, other2, rest3, *state))
    other3 = swap(rest3, "x")
    units = [(other2, 0, (2, 1, 1)), (side3, 0, (3, 1, 0))]
    *state, away = stage(units, state, second, last=True)
    late.append(swap(away, "core"))
    late_units.append(codes_of(units))

    peak = jnp.maximum(jnp.max(peaks), jnp.max(side0[half:]))
    peak = jnp.full((8, 128), peak.astype(F32))
    peak = jnp.maximum(peak, swap(peak, "core"))
    peak_ratio = (peak[0, 0] / limit).reshape(1)

    share = (total.astype(F32) * token_count ** (-0.5)).astype(BF16)
    other_share = swap(jnp.pad(share, ((0, 16), (0, 0))), "replica")
    other3, peak_ratio = lax.optimization_barrier((other3, peak_ratio))
    input_gradient, projected_keys = finish(
        where,
        scale,
        hidden,
        cotangent,
        (3, 1, 1),
        [other3, swap(other3, "core")],
        [state[0], swap(state[1], "core")],
        state[2],
        late,
        late_units,
    )
    weight_gradient = join(where, share, other_share)
    return (projected_keys, input_gradient, weight_gradient, peak_ratio)


def plain(hidden_states, key_weight, previous_peak, key_cotangent):
    names = ("replica", "x", "core")
    limit = previous_peak[0]
    unscale = limit / 448.0
    tokens, width = hidden_states.shape
    rows, features = key_weight.shape
    replicas = lax.axis_size("replica")
    nz, nx, nc = lax.axis_size("z"), lax.axis_size("x"), lax.axis_size("core")
    part = rows // replicas
    group = replicas * nx * nc
    split = hidden_states.reshape(tokens, nz, nx, nc, replicas, part)
    split = split.transpose(4, 2, 3, 0, 1, 5).reshape(group, tokens, nz * part)
    swapped = lax.all_to_all(split, names, 0, 0, tiled=True)
    cotangents = lax.all_gather(key_cotangent, names, axis=0, tiled=True)
    peak = lax.pmax(jnp.max(jnp.abs(key_weight.astype(F32))), ("z", "x", "core"))
    half = lax.dynamic_slice_in_dim(key_weight, lax.axis_index("replica") * part, part, 0)
    gathered = lax.all_gather(
        quantize(half, limit), ("z", "x", "core", "replica"), axis=0, tiled=True
    )
    keys_sum = jnp.dot(hidden_states, gathered, preferred_element_type=F32)
    grad_sum = lax.dot_general(
        key_cotangent, gathered, (((1,), (1,)), ((), ())), preferred_element_type=F32
    )
    term = lax.dot_general(
        swapped.reshape(group * tokens, nz * part),
        cotangents,
        (((0,), (0,)), ((), ())),
        preferred_element_type=F32,
    ).astype(BF16)
    total = lax.psum_scatter(term, "z", scatter_dimension=0, tiled=True).astype(F32)
    token_count = tokens * replicas * nz * nx * nc
    share = (total * token_count ** (-0.5)).astype(BF16)
    weight_gradient = lax.all_gather(share, "replica", axis=0, tiled=True)
    return (
        (keys_sum * unscale).astype(BF16),
        (grad_sum * unscale).astype(BF16),
        weight_gradient,
        (peak / limit).reshape(1),
    )


def solution(mesh):
    replicas, shards = mesh.shape["replica"], mesh.shape["fsdp"]
    grid = Mesh(mesh.devices.reshape(replicas, shards // 4, 2, 2), ("replica", "z", "x", "core"))
    fsdp = ("z", "x", "core")
    every = ("replica",) + fsdp
    in_specs = (P(every, None), P(fsdp, None), P(), P(every, None))
    out_specs = (P(every, None), P(every, None), P(fsdp, None), P())
    run = body if replicas == 2 and shards == 16 else plain
    return jax.shard_map(run, mesh=grid, in_specs=in_specs, out_specs=out_specs, check_vma=False)
```

```python
import functools

import jax
import jax.numpy as jnp
from jax import lax
from jax.experimental import pallas as pl
from jax.experimental.pallas import tpu as pltpu
from jax.sharding import Mesh
from jax.sharding import PartitionSpec as P

ANY = pl.BlockSpec(memory_space=pl.ANY)
SMEM = pl.BlockSpec(memory_space=pltpu.SMEM)
VMEM = pl.BlockSpec(memory_space=pltpu.VMEM)
PARAMS = pltpu.CompilerParams(vmem_limit_bytes=63 * 2**20)
CHEAP = pl.CostEstimate(flops=1, bytes_accessed=1, transcendentals=0)
F32, BF16 = jnp.float32, jnp.bfloat16


def quantize(weight, limit):
    return jnp.clip(weight.astype(F32) * (448.0 / limit), -448.0, 448.0).astype(BF16)


def swap(block, axis, mask=1):
    size = lax.axis_size(axis)
    return lax.ppermute(block, axis, [(i, i ^ mask) for i in range(size)])


def run(copies):
    for copy in copies:
        copy.start()
    for copy in copies:
        copy.wait()


def pack(core, hidden, rows, nz):
    tokens = hidden.shape[0]
    half = rows // 2
    group, blocks = 8, nz * 2

    def kernel(core_ref, hidden_ref, group_ref, other_ref, sem):
        copies = []
        for d in range(group):
            for k in range(nz):
                start = (k * 4 + d % 4) * rows + (d // 4) * half
                copies.append(
                    pltpu.make_async_copy(
                        hidden_ref.at[:, pl.ds(start, half)],
                        group_ref.at[d, :, pl.ds(k * half, half)],
                        sem.at[len(copies)],
                    )
                )
        for b in range(blocks):
            start = pl.multiple_of((b * 2 + 1 - core_ref[0]) * rows, rows)
            copies.append(
                pltpu.make_async_copy(
                    hidden_ref.at[:, pl.ds(start, rows)], other_ref.at[b], sem.at[len(copies)]
                )
            )
        run(copies)

    return pl.pallas_call(
        kernel,
        out_shape=[
            jax.ShapeDtypeStruct((group, tokens, nz * half), BF16),
            jax.ShapeDtypeStruct((blocks, tokens, rows), BF16),
        ],
        in_specs=[SMEM, ANY],
        out_specs=[VMEM, VMEM],
        scratch_shapes=[pltpu.SemaphoreType.DMA((group * nz + blocks,))],
        compiler_params=PARAMS,
        name="pack",
    )(core, hidden)


def weight_terms(slots, swapped, cotangents, tiles, state):
    sources, tokens, width = swapped.shape
    features = cotangents[0].shape[1]
    count = len(tiles)
    tile = width // 4

    def kernel(slots_ref, swapped_ref, *refs):
        cots_ref, refs = refs[:4], refs[4 + len(state) :]
        out_ref, lhs, rhs, out, sem, out_sem = refs
        shared = []
        for s in range(sources):
            place = pl.ds(pl.multiple_of(slots_ref[s] * tokens, tokens), tokens)
            source = cots_ref[s // 4].at[pl.ds(s % 4 * tokens, tokens)] if s % 4 < 3 else cots_ref[2 + s // 4]
            shared.append(pltpu.make_async_copy(source, rhs.at[place], sem.at[count, s]))
        loads = []
        for i, t in enumerate(tiles):
            at = pl.ds(t * tile, tile)
            places = [pl.ds(s * tokens, tokens) for s in range(sources)]
            loads.append(
                [
                    pltpu.make_async_copy(swapped_ref.at[s, :, at], lhs.at[i, place], sem.at[i, s])
                    for s, place in enumerate(places)
                ]
            )
        for copy in shared + loads[0]:
            copy.start()
        for copy in shared:
            copy.wait()
        stores = []
        for i, t in enumerate(tiles):
            for copy in loads[i]:
                copy.wait()
            for copy in loads[i + 1] if i + 1 < count else []:
                copy.start()
            out[i] = lax.dot_general(
                lhs[i], rhs[...], (((0,), (0,)), ((), ())), preferred_element_type=F32
            ).astype(BF16)
            target = out_ref.at[pl.ds(t * tile, tile)]
            stores.append(pltpu.make_async_copy(out.at[i], target, out_sem.at[i]))
            stores[-1].start()
        for copy in stores:
            copy.wait()

    return pl.pallas_call(
        kernel,
        out_shape=jax.ShapeDtypeStruct((width, features), BF16),
        in_specs=[SMEM] + [ANY] * (5 + len(state)),
        out_specs=ANY,
        input_output_aliases={6: 0} if state else {},
        scratch_shapes=[
            pltpu.VMEM((count, sources * tokens, tile), BF16),
            pltpu.VMEM((sources * tokens, features), BF16),
            pltpu.VMEM((count, tile, features), BF16),
            pltpu.SemaphoreType.DMA((count + 1, sources)),
            pltpu.SemaphoreType.DMA((count,)),
        ],
        cost_estimate=CHEAP,
        compiler_params=PARAMS,
        name="weight_terms",
    )(slots, swapped, *cotangents, *state)


def consume(where, scale, hidden, other, cotangents, units, state, arrived, last=False):
    tokens, width = hidden.shape
    rows, features = other.shape[2], cotangents[0].shape[1]
    half = rows // 2
    count = len(units)
    extra = len(arrived[1]) if arrived else 0
    chunks = [min(4, count - i) for i in range(0, count, 4)]
    arrays = []
    for array, _, _ in units:
        if not any(array is known for known in arrays):
            arrays.append(array)

    def kernel(where_ref, scale_ref, hidden_ref, other_ref, *refs):
        cots_ref, refs = refs[:2], refs[2:]
        array_refs, refs = refs[: len(arrays)], refs[len(arrays) :]
        if state:
            totals_ref, refs = refs[:2], refs[3:]
        arrived_refs, refs = refs[: (extra + 3) // 4], refs[(extra + 3) // 4 :]
        total_refs, gradient_ref, away_refs, refs = refs[:2], refs[2], refs[3 : 3 + len(chunks)], refs[3 + len(chunks) :]
        hid, cot, wgt, acc, prior, near, far, held, sent, sem, cot_sem, out_sem, near_sem, far_sem = refs
        place = functools.partial(unit_columns, where_ref, rows)
        early = []
        for s in range(2):
            span = pl.ds(s * tokens, tokens)
            source = cots_ref[s].at[pl.ds(0, tokens)]
            early.append(pltpu.make_async_copy(source, cot.at[span], cot_sem.at[s]))
        for copy in early:
            copy.start()
        loads = []
        for b, (array, row, (k, side, part)) in enumerate(units):
            ref = [r for r, known in zip(array_refs, arrays) if known is array][0]
            at = pl.multiple_of((1 - where_ref[2] if part else where_ref[2]) * half, half)
            source = ref.at[where_ref[3] ^ k] if row is None else ref.at[pl.ds(row, half)]
            block = (where_ref[3] ^ k) * 2 + (1 - where_ref[1] if side else where_ref[1])
            pairs = [
                (source, wgt.at[b]),
                (hidden_ref.at[:, place((k, side, part), 0)], hid.at[b, pl.ds(0, tokens)]),
                (other_ref.at[block, :, pl.ds(at, half)], hid.at[b, pl.ds(tokens, tokens)]),
            ]
            loads.append([pltpu.make_async_copy(f, t, sem.at[i, b]) for i, (f, t) in enumerate(pairs)])
            for copy in loads[-1]:
                copy.start()
        before = []
        for i, ref in enumerate(arrived_refs):
            size = min(4, extra - 4 * i)
            before.append(pltpu.make_async_copy(ref, held.at[pl.ds(4 * i, size)], cot_sem.at[4 + i]))
        if state:
            for s in range(2):
                span = pl.ds(s * tokens, tokens)
                before.append(pltpu.make_async_copy(totals_ref[s], prior.at[span], cot_sem.at[2 + s]))
        for copy in before:
            copy.start()
        for copy in early:
            copy.wait()
        acc[...] = jnp.zeros_like(acc)

        def step(b, carry):
            for i, ref in enumerate((wgt.at[b], hid.at[b, pl.ds(0, tokens)], hid.at[b, pl.ds(0, tokens)])):
                pltpu.make_async_copy(ref, ref, sem.at[i, b]).wait()
            weight = wgt[b]
            acc[...] += jnp.dot(hid[b], weight, preferred_element_type=F32)
            product = (
                lax.dot_general(
                    cot[...], weight, (((1,), (1,)), ((), ())), preferred_element_type=F32
                )
                * scale_ref[0]
            ).astype(BF16)
            near[b] = product[:tokens]
            far[b] = product[tokens:]
            return carry

        lax.fori_loop(0, count, step, 0)
        late = [
            pltpu.make_async_copy(far.at[pl.ds(4 * i, size)], away_refs[i], far_sem.at[i])
            for i, size in enumerate(chunks)
        ]
        for b, (_, _, unit) in enumerate(units):
            late.append(
                pltpu.make_async_copy(near.at[b], gradient_ref.at[:, place(unit, 0)], near_sem.at[b])
            )
        for copy in late:
            copy.start()
        for copy in before:
            copy.wait()
        if state:
            acc[...] += prior[...]
        sums = [acc.at[pl.ds(s * tokens, tokens)] for s in range(2)]
        if last:
            sent[...] = acc[pl.ds(tokens, tokens)].astype(BF16)
            sums[1] = sent
        end = [pltpu.make_async_copy(sums[s], total_refs[s], out_sem.at[s]) for s in range(2)]
        for e in range(extra):
            columns = place(arrived[1][e], 1)
            end.append(
                pltpu.make_async_copy(held.at[e], gradient_ref.at[:, columns], out_sem.at[2 + e])
            )
        for copy in end:
            copy.start()
        for copy in late + end:
            copy.wait()

    sums = jax.ShapeDtypeStruct((tokens, features), F32)
    operands = [where, scale, hidden, other, *cotangents, *arrays, *state]
    if arrived:
        operands += arrived[0]
    return pl.pallas_call(
        kernel,
        out_shape=[
            sums,
            jax.ShapeDtypeStruct(sums.shape, BF16) if last else sums,
            jax.ShapeDtypeStruct((tokens, width), BF16),
            *[jax.ShapeDtypeStruct((size, tokens, half), BF16) for size in chunks],
        ],
        in_specs=[SMEM, SMEM] + [ANY] * (len(operands) - 2),
        out_specs=[ANY] * (3 + len(chunks)),
        input_output_aliases=(
            {6 + len(arrays) + i: i for i in (0, 2) + (() if last else (1,))} if state else {}
        ),
        scratch_shapes=[
            pltpu.VMEM((count, 2 * tokens, half), BF16),
            pltpu.VMEM((2 * tokens, features), BF16),
            pltpu.VMEM((count, half, features), BF16),
            pltpu.VMEM((2 * tokens, features), F32),
            pltpu.VMEM((2 * tokens, features) if state else (8, 128), F32),
            pltpu.VMEM((count, tokens, half), BF16),
            pltpu.VMEM((count, tokens, half), BF16),
            pltpu.VMEM((max(extra, 1), tokens, half), BF16),
            pltpu.VMEM((tokens, features) if last else (16, 128), BF16),
            pltpu.SemaphoreType.DMA((3, count)),
            pltpu.SemaphoreType.DMA((4 + (extra + 3) // 4,)),
            pltpu.SemaphoreType.DMA((2 + extra,)),
            pltpu.SemaphoreType.DMA((count,)),
            pltpu.SemaphoreType.DMA((len(chunks),)),
        ],
        cost_estimate=CHEAP,
        compiler_params=PARAMS,
        name="consume",
    )(*operands)


def unit_columns(where_ref, rows, unit, core):
    k, side, part = unit
    half = rows // 2
    x = 1 - where_ref[1] if side else where_ref[1]
    c = 1 - where_ref[0] if core else where_ref[0]
    r = 1 - where_ref[2] if part else where_ref[2]
    at = (((where_ref[3] ^ k) * 2 + x) * 2 + c) * rows + r * half
    return pl.ds(pl.multiple_of(at, half), half)


def finish(where, scale, hidden, cotangent, unit, weights, sums, gradient, arrived, units):
    tokens, width = hidden.shape
    half, features = weights[0].shape
    counts = [len(some) for some in units]

    def kernel(where_ref, scale_ref, hidden_ref, cot_ref, *refs):
        weight_refs, sum_refs, arrived_refs, refs = refs[:2], refs[2:4], refs[4 : 4 + len(units)], refs[5 + len(units) :]
        gradient_ref, keys_ref, hid, cot, wgt, near, far, held, new, sem, held_sem, out_sem = refs
        place = functools.partial(unit_columns, where_ref, 2 * half)
        loads = [pltpu.make_async_copy(cot_ref, cot, sem.at[0])]
        for i in range(2):
            loads.append(pltpu.make_async_copy(weight_refs[i], wgt.at[i], sem.at[1 + i]))
            columns = hidden_ref.at[:, place(unit, i)]
            loads.append(pltpu.make_async_copy(columns, hid.at[i], sem.at[3 + i]))
        loads.append(pltpu.make_async_copy(sum_refs[0], near, sem.at[5]))
        loads.append(pltpu.make_async_copy(sum_refs[1], far, sem.at[6]))
        for copy in loads:
            copy.start()
        fills, stores = [], []
        for j, (ref, some) in enumerate(zip(arrived_refs, units)):
            first = sum(counts[:j])
            fills.append(pltpu.make_async_copy(ref, held.at[pl.ds(first, len(some))], held_sem.at[j]))
            fills[-1].start()
            for e, one in enumerate(some):
                target = gradient_ref.at[:, place(one, 1)]
                stores.append(pltpu.make_async_copy(held.at[first + e], target, out_sem.at[2 + first + e]))
        for copy in loads[:5]:
            copy.wait()
        for i in range(2):
            new[i] = (
                lax.dot_general(
                    cot[...], wgt[i], (((1,), (1,)), ((), ())), preferred_element_type=F32
                )
                * scale_ref[0]
            ).astype(BF16)
            target = gradient_ref.at[:, place(unit, i)]
            stores.append(pltpu.make_async_copy(new.at[i], target, out_sem.at[i]))
            stores[-1].start()
        for copy in fills:
            copy.wait()
        for copy in stores[:-2]:
            copy.start()
        total = jnp.dot(hid[0], wgt[0], preferred_element_type=F32)
        total += jnp.dot(hid[1], wgt[1], preferred_element_type=F32)
        for copy in loads[5:]:
            copy.wait()
        keys_ref[...] = ((total + near[...] + far[...].astype(F32)) * scale_ref[0]).astype(BF16)
        for copy in stores:
            copy.wait()

    return pl.pallas_call(
        kernel,
        out_shape=[
            jax.ShapeDtypeStruct(gradient.shape, BF16),
            jax.ShapeDtypeStruct((tokens, features), BF16),
        ],
        in_specs=[SMEM, SMEM] + [ANY] * (7 + len(units)),
        out_specs=[ANY, VMEM],
        input_output_aliases={8 + len(units): 0},
        scratch_shapes=[
            pltpu.VMEM((2, tokens, half), BF16),
            pltpu.VMEM((tokens, features), BF16),
            pltpu.VMEM((2, half, features), BF16),
            pltpu.VMEM((tokens, features), F32),
            pltpu.VMEM((tokens, features), BF16),
            pltpu.VMEM((sum(counts), tokens, half), BF16),
            pltpu.VMEM((2, tokens, half), BF16),
            pltpu.SemaphoreType.DMA((7,)),
            pltpu.SemaphoreType.DMA((len(units),)),
            pltpu.SemaphoreType.DMA((2 + sum(counts),)),
        ],
        cost_estimate=CHEAP,
        compiler_params=PARAMS,
        name="finish",
    )(where, scale, hidden, cotangent, *weights, *sums, *arrived, gradient)


def join(where, mine, theirs):
    half, features = mine.shape[0] - 16, mine.shape[1]

    def kernel(where_ref, mine_ref, theirs_ref, out_ref):
        at = pl.multiple_of(where_ref[2] * half, half)
        out_ref[pl.ds(at, half), :] = mine_ref[pl.ds(0, half), :]
        out_ref[pl.ds(half - at, half), :] = theirs_ref[pl.ds(0, half), :]

    return pl.pallas_call(
        kernel,
        out_shape=jax.ShapeDtypeStruct((2 * half, features), BF16),
        in_specs=[SMEM, VMEM, VMEM],
        out_specs=VMEM,
        compiler_params=PARAMS,
        name="join",
    )(where, mine, theirs)


def body(hidden, key_weight, previous_peak, cotangent):
    limit = previous_peak[0]
    unscale = limit / 448.0
    scale = unscale.reshape(1)
    tokens = hidden.shape[0]
    rows = key_weight.shape[0]
    r, z, x, c = (lax.axis_index(name) for name in ("replica", "z", "x", "core"))
    where = jnp.stack([c, x, r, z]).astype(jnp.int32)
    nz = lax.axis_size("z")
    token_count = tokens * lax.axis_size(("replica", "z", "x", "core"))

    half = rows // 2
    own = quantize(lax.dynamic_slice_in_dim(key_weight, r * half, half, 0), limit)
    rest = quantize(lax.dynamic_slice_in_dim(key_weight, (1 - r) * half, half, 0), limit)
    hidden, own, rest = lax.optimization_barrier((hidden, own, rest))
    mine = lax.all_gather(own, "z", axis=0)
    rest0, mine = lax.optimization_barrier((rest, mine))
    rest1, rest2 = swap(rest0, "z", 1), swap(rest0, "z", 2)

    cots = [swap(cotangent, "x"), swap(cotangent, "replica")]
    for_group, for_other = pack(where, hidden, rows, nz)
    for_group, *cots = lax.optimization_barrier((for_group, *cots))
    swapped = lax.all_to_all(for_group, ("replica", "x", "core"), 0, 0, tiled=True)
    cut = tokens // 2
    diagonal = [swap(cots[1][:cut], "x"), swap(cots[0][cut:], "replica")]
    peaks = jnp.max(jnp.abs(key_weight), axis=0, keepdims=True)
    peaks = jnp.broadcast_to(peaks, (16, peaks.shape[1]))
    for k in (1, 2):
        peaks = jnp.maximum(peaks, swap(peaks, "z", k))
    cots = jnp.concatenate([cotangent, *cots], axis=0)
    cots, peaks = lax.optimization_barrier((cots, peaks))
    cots = [cots, swap(cots, "core")]
    rest1, rest2, *diagonal = lax.optimization_barrier((rest1, rest2, *diagonal))
    diagonal = jnp.concatenate(diagonal, axis=0)
    diagonal = [diagonal, swap(diagonal, "core")]
    slots = [
        ((r ^ dr) * 2 + (x ^ dx)) * 2 + (c ^ dc) for dc in (0, 1) for dr in (0, 1) for dx in (0, 1)
    ]
    slots = jnp.stack(slots).astype(jnp.int32)
    other = swap(for_other, "core")

    parts = [jnp.concatenate([own, peaks])]
    parts += [lax.dynamic_index_in_dim(mine, z ^ k, keepdims=False) for k in (1, 2, 3)]
    cots[1], *parts = lax.optimization_barrier((cots[1], *parts))
    side0 = swap(parts[0], "x")
    rest3 = swap(jnp.concatenate([parts[3], peaks]), "replica")
    swapped, other = lax.optimization_barrier((swapped, other))
    term = weight_terms(slots, swapped, cots + diagonal, (0, 1, 2, 3), [])
    stage = functools.partial(consume, where, scale, hidden, other, [cotangent, cots[1]])

    def codes_of(units):
        return [unit for _, _, unit in units]

    term, side0, rest3, *parts = lax.optimization_barrier((term, side0, rest3, *parts))
    rest3 = rest3[:half]
    total = lax.psum_scatter(term, "z", scatter_dimension=0, tiled=True)
    side1, other0 = swap(parts[1], "x"), swap(side0, "replica")
    units = [(own, 0, (0, 0, 0)), (rest0, 0, (0, 0, 1))] + [(mine, None, (k, 0, 0)) for k in (1, 2, 3)]
    *state, away0, away1 = stage(units, [], None)
    first = ([swap(away0, "core"), swap(away1, "core")], codes_of(units))

    side1, other0, *rest = lax.optimization_barrier((side1, other0, *state, *parts))
    state, parts = rest[:3], rest[3:]
    side2, other1 = swap(parts[2], "x"), swap(side1, "replica")
    units = [(side0, 0, (0, 1, 0)), (other0, 0, (0, 1, 1)), (side1, 0, (1, 1, 0)), (rest1, 0, (1, 0, 1))]
    *state, away = stage(units, state, None)
    second = ([swap(away, "core")], codes_of(units))

    peak = jnp.maximum(jnp.max(peaks), jnp.max(side0[half:]))
    peak = jnp.full((8, 128), peak.astype(F32))
    peak = jnp.maximum(peak, swap(peak, "core"))
    peak_ratio = (peak[0, 0] / limit).reshape(1)

    side2, other1, peak_ratio, *rest = lax.optimization_barrier((side2, other1, peak_ratio, *state, *parts))
    state, parts = rest[:3], rest[3:]
    side3, other2 = swap(parts[3], "x"), swap(side2, "replica")
    units = [(rest2, 0, (2, 0, 1)), (rest3, 0, (3, 0, 1)), (other1, 0, (1, 1, 1)), (side2, 0, (2, 1, 0))]
    *state, away = stage(units, state, first)
    late, late_units = [swap(away, "core")], [codes_of(units)]

    side3, other2, rest3, *state = lax.optimization_barrier((side3, other2, rest3, *state))
    other3 = swap(rest3, "x")
    units = [(other2, 0, (2, 1, 1)), (side3, 0, (3, 1, 0))]
    *state, away = stage(units, state, second, last=True)
    late.append(swap(away, "core"))
    late_units.append(codes_of(units))

    share = jnp.pad((total.astype(F32) * token_count ** (-0.5)).astype(BF16), ((0, 16), (0, 0)))
    other_share = swap(share, "replica")
    input_gradient, projected_keys = finish(
        where,
        scale,
        hidden,
        cotangent,
        (3, 1, 1),
        [other3, swap(other3, "core")],
        [state[0], swap(state[1], "core")],
        state[2],
        late,
        late_units,
    )
    weight_gradient = join(where, share, other_share)
    return (projected_keys, input_gradient, weight_gradient, peak_ratio)


def plain(hidden_states, key_weight, previous_peak, key_cotangent):
    names = ("replica", "x", "core")
    limit = previous_peak[0]
    unscale = limit / 448.0
    tokens, width = hidden_states.shape
    rows, features = key_weight.shape
    replicas = lax.axis_size("replica")
    nz, nx, nc = lax.axis_size("z"), lax.axis_size("x"), lax.axis_size("core")
    part = rows // replicas
    group = replicas * nx * nc
    split = hidden_states.reshape(tokens, nz, nx, nc, replicas, part)
    split = split.transpose(4, 2, 3, 0, 1, 5).reshape(group, tokens, nz * part)
    swapped = lax.all_to_all(split, names, 0, 0, tiled=True)
    cotangents = lax.all_gather(key_cotangent, names, axis=0, tiled=True)
    peak = lax.pmax(jnp.max(jnp.abs(key_weight.astype(F32))), ("z", "x", "core"))
    half = lax.dynamic_slice_in_dim(key_weight, lax.axis_index("replica") * part, part, 0)
    gathered = lax.all_gather(
        quantize(half, limit), ("z", "x", "core", "replica"), axis=0, tiled=True
    )
    keys_sum = jnp.dot(hidden_states, gathered, preferred_element_type=F32)
    grad_sum = lax.dot_general(
        key_cotangent, gathered, (((1,), (1,)), ((), ())), preferred_element_type=F32
    )
    term = lax.dot_general(
        swapped.reshape(group * tokens, nz * part),
        cotangents,
        (((0,), (0,)), ((), ())),
        preferred_element_type=F32,
    ).astype(BF16)
    total = lax.psum_scatter(term, "z", scatter_dimension=0, tiled=True).astype(F32)
    token_count = tokens * replicas * nz * nx * nc
    share = (total * token_count ** (-0.5)).astype(BF16)
    weight_gradient = lax.all_gather(share, "replica", axis=0, tiled=True)
    return (
        (keys_sum * unscale).astype(BF16),
        (grad_sum * unscale).astype(BF16),
        weight_gradient,
        (peak / limit).reshape(1),
    )


def solution(mesh):
    replicas, shards = mesh.shape["replica"], mesh.shape["fsdp"]
    grid = Mesh(mesh.devices.reshape(replicas, shards // 4, 2, 2), ("replica", "z", "x", "core"))
    fsdp = ("z", "x", "core")
    every = ("replica",) + fsdp
    in_specs = (P(every, None), P(fsdp, None), P(), P(every, None))
    out_specs = (P(every, None), P(every, None), P(fsdp, None), P())
    run = body if replicas == 2 and shards == 16 else plain
    return jax.shard_map(run, mesh=grid, in_specs=in_specs, out_specs=out_specs, check_vma=False)
```

```python
import functools

import jax
import jax.numpy as jnp
from jax import lax
from jax.experimental import pallas as pl
from jax.experimental.pallas import tpu as pltpu
from jax.sharding import Mesh
from jax.sharding import PartitionSpec as P

ANY = pl.BlockSpec(memory_space=pl.ANY)
SMEM = pl.BlockSpec(memory_space=pltpu.SMEM)
VMEM = pl.BlockSpec(memory_space=pltpu.VMEM)
PARAMS = pltpu.CompilerParams(vmem_limit_bytes=63 * 2**20)
CHEAP = pl.CostEstimate(flops=1, bytes_accessed=1, transcendentals=0)
F32, BF16 = jnp.float32, jnp.bfloat16


def quantize(weight, limit):
    return jnp.clip(weight.astype(F32) * (448.0 / limit), -448.0, 448.0).astype(BF16)


def swap(block, axis, mask=1):
    size = lax.axis_size(axis)
    return lax.ppermute(block, axis, [(i, i ^ mask) for i in range(size)])


def run(copies):
    for copy in copies:
        copy.start()
    for copy in copies:
        copy.wait()


def pack(core, hidden, rows, nz):
    tokens = hidden.shape[0]
    half = rows // 2
    group, blocks = 8, nz * 2

    def kernel(core_ref, hidden_ref, group_ref, other_ref, sem):
        copies = []
        for d in range(group):
            for k in range(nz):
                start = (k * 4 + d % 4) * rows + (d // 4) * half
                copies.append(
                    pltpu.make_async_copy(
                        hidden_ref.at[:, pl.ds(start, half)],
                        group_ref.at[d, :, pl.ds(k * half, half)],
                        sem.at[len(copies)],
                    )
                )
        for b in range(blocks):
            start = pl.multiple_of((b * 2 + 1 - core_ref[0]) * rows, rows)
            copies.append(
                pltpu.make_async_copy(
                    hidden_ref.at[:, pl.ds(start, rows)], other_ref.at[b], sem.at[len(copies)]
                )
            )
        run(copies)

    return pl.pallas_call(
        kernel,
        out_shape=[
            jax.ShapeDtypeStruct((group, tokens, nz * half), BF16),
            jax.ShapeDtypeStruct((blocks, tokens, rows), BF16),
        ],
        in_specs=[SMEM, ANY],
        out_specs=[VMEM, VMEM],
        scratch_shapes=[pltpu.SemaphoreType.DMA((group * nz + blocks,))],
        compiler_params=PARAMS,
        name="pack",
    )(core, hidden)


def weight_terms(slots, swapped, cotangents, tiles, state):
    sources, tokens, width = swapped.shape
    features = cotangents[0].shape[1]
    count = len(tiles)
    tile = width // 4

    def kernel(slots_ref, swapped_ref, *refs):
        cots_ref, refs = refs[:4], refs[4 + len(state) :]
        out_ref, lhs, rhs, out, sem, out_sem = refs
        copies = []
        for s in range(sources):
            place = pl.ds(pl.multiple_of(slots_ref[s] * tokens, tokens), tokens)
            source = cots_ref[s // 4].at[pl.ds(s % 4 * tokens, tokens)] if s % 4 < 3 else cots_ref[2 + s // 4]
            copies.append(pltpu.make_async_copy(source, rhs.at[place], sem.at[count, s]))
        for i, t in enumerate(tiles):
            at = pl.ds(t * tile, tile)
            for s in range(sources):
                place = pl.ds(s * tokens, tokens)
                copies.append(
                    pltpu.make_async_copy(swapped_ref.at[s, :, at], lhs.at[i, place], sem.at[i, s])
                )
        for copy in copies:
            copy.start()
        stores = []
        for i, t in enumerate(tiles):
            for copy in copies[(i + 1 if i else 0) * sources : (i + 2) * sources]:
                copy.wait()
            out[i] = lax.dot_general(
                lhs[i], rhs[...], (((0,), (0,)), ((), ())), preferred_element_type=F32
            ).astype(BF16)
            target = out_ref.at[pl.ds(t * tile, tile)]
            stores.append(pltpu.make_async_copy(out.at[i], target, out_sem.at[i]))
            stores[-1].start()
        for copy in stores:
            copy.wait()

    return pl.pallas_call(
        kernel,
        out_shape=jax.ShapeDtypeStruct((width, features), BF16),
        in_specs=[SMEM] + [ANY] * (5 + len(state)),
        out_specs=ANY,
        input_output_aliases={6: 0} if state else {},
        scratch_shapes=[
            pltpu.VMEM((count, sources * tokens, tile), BF16),
            pltpu.VMEM((sources * tokens, features), BF16),
            pltpu.VMEM((count, tile, features), BF16),
            pltpu.SemaphoreType.DMA((count + 1, sources)),
            pltpu.SemaphoreType.DMA((count,)),
        ],
        cost_estimate=CHEAP,
        compiler_params=PARAMS,
        name="weight_terms",
    )(slots, swapped, *cotangents, *state)


def consume(where, scale, hidden, other, cotangents, units, state, arrived, last=False):
    tokens, width = hidden.shape
    rows, features = other.shape[2], cotangents[0].shape[1]
    half = rows // 2
    count = len(units)
    extra = len(arrived[1]) if arrived else 0
    chunks = [min(4, count - i) for i in range(0, count, 4)]
    arrays = []
    for array, _, _ in units:
        if not any(array is known for known in arrays):
            arrays.append(array)

    def kernel(where_ref, scale_ref, hidden_ref, other_ref, *refs):
        cots_ref, refs = refs[:2], refs[2:]
        array_refs, refs = refs[: len(arrays)], refs[len(arrays) :]
        if state:
            totals_ref, refs = refs[:2], refs[3:]
        arrived_refs, refs = refs[: (extra + 3) // 4], refs[(extra + 3) // 4 :]
        total_refs, gradient_ref, away_refs, refs = refs[:2], refs[2], refs[3 : 3 + len(chunks)], refs[3 + len(chunks) :]
        hid, cot, wgt, acc, prior, near, far, held, sent, sem, cot_sem, out_sem, near_sem, far_sem = refs
        place = functools.partial(unit_columns, where_ref, rows)
        early = []
        for s in range(2):
            span = pl.ds(s * tokens, tokens)
            source = cots_ref[s].at[pl.ds(0, tokens)]
            early.append(pltpu.make_async_copy(source, cot.at[span], cot_sem.at[s]))
        for copy in early:
            copy.start()
        loads = []
        for b, (array, row, (k, side, part)) in enumerate(units):
            ref = [r for r, known in zip(array_refs, arrays) if known is array][0]
            at = pl.multiple_of((1 - where_ref[2] if part else where_ref[2]) * half, half)
            source = ref.at[where_ref[3] ^ k] if row is None else ref.at[pl.ds(row, half)]
            block = (where_ref[3] ^ k) * 2 + (1 - where_ref[1] if side else where_ref[1])
            pairs = [
                (source, wgt.at[b]),
                (hidden_ref.at[:, place((k, side, part), 0)], hid.at[b, pl.ds(0, tokens)]),
                (other_ref.at[block, :, pl.ds(at, half)], hid.at[b, pl.ds(tokens, tokens)]),
            ]
            loads.append([pltpu.make_async_copy(f, t, sem.at[i, b]) for i, (f, t) in enumerate(pairs)])
            for copy in loads[-1]:
                copy.start()
        before = []
        for i, ref in enumerate(arrived_refs):
            size = min(4, extra - 4 * i)
            before.append(pltpu.make_async_copy(ref, held.at[pl.ds(4 * i, size)], cot_sem.at[4 + i]))
        if state:
            for s in range(2):
                span = pl.ds(s * tokens, tokens)
                before.append(pltpu.make_async_copy(totals_ref[s], prior.at[span], cot_sem.at[2 + s]))
        for copy in before:
            copy.start()
        for copy in early:
            copy.wait()
        acc[...] = jnp.zeros_like(acc)

        def step(b, carry):
            for i, ref in enumerate((wgt.at[b], hid.at[b, pl.ds(0, tokens)], hid.at[b, pl.ds(0, tokens)])):
                pltpu.make_async_copy(ref, ref, sem.at[i, b]).wait()
            weight = wgt[b]
            acc[...] += jnp.dot(hid[b], weight, preferred_element_type=F32)
            product = (
                lax.dot_general(
                    cot[...], weight, (((1,), (1,)), ((), ())), preferred_element_type=F32
                )
                * scale_ref[0]
            ).astype(BF16)
            near[b] = product[:tokens]
            far[b] = product[tokens:]
            return carry

        lax.fori_loop(0, count, step, 0)
        late = [
            pltpu.make_async_copy(far.at[pl.ds(4 * i, size)], away_refs[i], far_sem.at[i])
            for i, size in enumerate(chunks)
        ]
        for b, (_, _, unit) in enumerate(units):
            late.append(
                pltpu.make_async_copy(near.at[b], gradient_ref.at[:, place(unit, 0)], near_sem.at[b])
            )
        for copy in late:
            copy.start()
        for copy in before:
            copy.wait()
        if state:
            acc[...] += prior[...]
        sums = [acc.at[pl.ds(s * tokens, tokens)] for s in range(2)]
        if last:
            sent[...] = acc[pl.ds(tokens, tokens)].astype(BF16)
            sums[1] = sent
        end = [pltpu.make_async_copy(sums[s], total_refs[s], out_sem.at[s]) for s in range(2)]
        for e in range(extra):
            columns = place(arrived[1][e], 1)
            end.append(
                pltpu.make_async_copy(held.at[e], gradient_ref.at[:, columns], out_sem.at[2 + e])
            )
        for copy in end:
            copy.start()
        for copy in late + end:
            copy.wait()

    sums = jax.ShapeDtypeStruct((tokens, features), F32)
    operands = [where, scale, hidden, other, *cotangents, *arrays, *state]
    if arrived:
        operands += arrived[0]
    return pl.pallas_call(
        kernel,
        out_shape=[
            sums,
            jax.ShapeDtypeStruct(sums.shape, BF16) if last else sums,
            jax.ShapeDtypeStruct((tokens, width), BF16),
            *[jax.ShapeDtypeStruct((size, tokens, half), BF16) for size in chunks],
        ],
        in_specs=[SMEM, SMEM] + [ANY] * (len(operands) - 2),
        out_specs=[ANY] * (3 + len(chunks)),
        input_output_aliases=(
            {6 + len(arrays) + i: i for i in (0, 2) + (() if last else (1,))} if state else {}
        ),
        scratch_shapes=[
            pltpu.VMEM((count, 2 * tokens, half), BF16),
            pltpu.VMEM((2 * tokens, features), BF16),
            pltpu.VMEM((count, half, features), BF16),
            pltpu.VMEM((2 * tokens, features), F32),
            pltpu.VMEM((2 * tokens, features) if state else (8, 128), F32),
            pltpu.VMEM((count, tokens, half), BF16),
            pltpu.VMEM((count, tokens, half), BF16),
            pltpu.VMEM((max(extra, 1), tokens, half), BF16),
            pltpu.VMEM((tokens, features) if last else (16, 128), BF16),
            pltpu.SemaphoreType.DMA((3, count)),
            pltpu.SemaphoreType.DMA((4 + (extra + 3) // 4,)),
            pltpu.SemaphoreType.DMA((2 + extra,)),
            pltpu.SemaphoreType.DMA((count,)),
            pltpu.SemaphoreType.DMA((len(chunks),)),
        ],
        cost_estimate=CHEAP,
        compiler_params=PARAMS,
        name="consume",
    )(*operands)


def unit_columns(where_ref, rows, unit, core):
    k, side, part = unit
    half = rows // 2
    x = 1 - where_ref[1] if side else where_ref[1]
    c = 1 - where_ref[0] if core else where_ref[0]
    r = 1 - where_ref[2] if part else where_ref[2]
    at = (((where_ref[3] ^ k) * 2 + x) * 2 + c) * rows + r * half
    return pl.ds(pl.multiple_of(at, half), half)


def finish(where, scale, hidden, cotangent, unit, weights, sums, gradient, arrived, units):
    tokens, width = hidden.shape
    half, features = weights[0].shape
    counts = [len(some) for some in units]

    def kernel(where_ref, scale_ref, hidden_ref, cot_ref, *refs):
        weight_refs, sum_refs, arrived_refs, refs = refs[:2], refs[2:4], refs[4 : 4 + len(units)], refs[5 + len(units) :]
        gradient_ref, keys_ref, hid, cot, wgt, near, far, held, new, sem, held_sem, out_sem = refs
        place = functools.partial(unit_columns, where_ref, 2 * half)
        loads = [pltpu.make_async_copy(cot_ref, cot, sem.at[0])]
        for i in range(2):
            loads.append(pltpu.make_async_copy(weight_refs[i], wgt.at[i], sem.at[1 + i]))
            columns = hidden_ref.at[:, place(unit, i)]
            loads.append(pltpu.make_async_copy(columns, hid.at[i], sem.at[3 + i]))
        loads.append(pltpu.make_async_copy(sum_refs[0], near, sem.at[5]))
        loads.append(pltpu.make_async_copy(sum_refs[1], far, sem.at[6]))
        for copy in loads:
            copy.start()
        fills, stores = [], []
        for j, (ref, some) in enumerate(zip(arrived_refs, units)):
            first = sum(counts[:j])
            fills.append(pltpu.make_async_copy(ref, held.at[pl.ds(first, len(some))], held_sem.at[j]))
            fills[-1].start()
            for e, one in enumerate(some):
                target = gradient_ref.at[:, place(one, 1)]
                stores.append(pltpu.make_async_copy(held.at[first + e], target, out_sem.at[2 + first + e]))
        for copy in loads[:5]:
            copy.wait()
        for i in range(2):
            new[i] = (
                lax.dot_general(
                    cot[...], wgt[i], (((1,), (1,)), ((), ())), preferred_element_type=F32
                )
                * scale_ref[0]
            ).astype(BF16)
            target = gradient_ref.at[:, place(unit, i)]
            stores.append(pltpu.make_async_copy(new.at[i], target, out_sem.at[i]))
            stores[-1].start()
        for copy in fills:
            copy.wait()
        for copy in stores[:-2]:
            copy.start()
        total = jnp.dot(hid[0], wgt[0], preferred_element_type=F32)
        total += jnp.dot(hid[1], wgt[1], preferred_element_type=F32)
        for copy in loads[5:]:
            copy.wait()
        keys_ref[...] = ((total + near[...] + far[...].astype(F32)) * scale_ref[0]).astype(BF16)
        for copy in stores:
            copy.wait()

    return pl.pallas_call(
        kernel,
        out_shape=[
            jax.ShapeDtypeStruct(gradient.shape, BF16),
            jax.ShapeDtypeStruct((tokens, features), BF16),
        ],
        in_specs=[SMEM, SMEM] + [ANY] * (7 + len(units)),
        out_specs=[ANY, VMEM],
        input_output_aliases={8 + len(units): 0},
        scratch_shapes=[
            pltpu.VMEM((2, tokens, half), BF16),
            pltpu.VMEM((tokens, features), BF16),
            pltpu.VMEM((2, half, features), BF16),
            pltpu.VMEM((tokens, features), F32),
            pltpu.VMEM((tokens, features), BF16),
            pltpu.VMEM((sum(counts), tokens, half), BF16),
            pltpu.VMEM((2, tokens, half), BF16),
            pltpu.SemaphoreType.DMA((7,)),
            pltpu.SemaphoreType.DMA((len(units),)),
            pltpu.SemaphoreType.DMA((2 + sum(counts),)),
        ],
        cost_estimate=CHEAP,
        compiler_params=PARAMS,
        name="finish",
    )(where, scale, hidden, cotangent, *weights, *sums, *arrived, gradient)


def join(where, mine, theirs):
    half, features = mine.shape[0] - 16, mine.shape[1]

    def kernel(where_ref, mine_ref, theirs_ref, out_ref):
        at = pl.multiple_of(where_ref[2] * half, half)
        out_ref[pl.ds(at, half), :] = mine_ref[pl.ds(0, half), :]
        out_ref[pl.ds(half - at, half), :] = theirs_ref[pl.ds(0, half), :]

    return pl.pallas_call(
        kernel,
        out_shape=jax.ShapeDtypeStruct((2 * half, features), BF16),
        in_specs=[SMEM, VMEM, VMEM],
        out_specs=VMEM,
        compiler_params=PARAMS,
        name="join",
    )(where, mine, theirs)


def body(hidden, key_weight, previous_peak, cotangent):
    limit = previous_peak[0]
    unscale = limit / 448.0
    scale = unscale.reshape(1)
    tokens = hidden.shape[0]
    rows = key_weight.shape[0]
    r, z, x, c = (lax.axis_index(name) for name in ("replica", "z", "x", "core"))
    where = jnp.stack([c, x, r, z]).astype(jnp.int32)
    nz = lax.axis_size("z")
    token_count = tokens * lax.axis_size(("replica", "z", "x", "core"))

    half = rows // 2
    own = quantize(lax.dynamic_slice_in_dim(key_weight, r * half, half, 0), limit)
    rest = quantize(lax.dynamic_slice_in_dim(key_weight, (1 - r) * half, half, 0), limit)
    hidden, own, rest = lax.optimization_barrier((hidden, own, rest))
    mine = lax.all_gather(own, "z", axis=0)
    rest0, mine = lax.optimization_barrier((rest, mine))
    rest1, rest2 = swap(rest0, "z", 1), swap(rest0, "z", 2)

    cots = [swap(cotangent, "x"), swap(cotangent, "replica")]
    for_group, for_other = pack(where, hidden, rows, nz)
    for_group, *cots = lax.optimization_barrier((for_group, *cots))
    swapped = lax.all_to_all(for_group, ("replica", "x", "core"), 0, 0, tiled=True)
    cut = tokens // 2
    diagonal = [swap(cots[1][:cut], "x"), swap(cots[0][cut:], "replica")]
    peaks = jnp.max(jnp.abs(key_weight), axis=0, keepdims=True)
    peaks = jnp.broadcast_to(peaks, (16, peaks.shape[1]))
    for k in (1, 2):
        peaks = jnp.maximum(peaks, swap(peaks, "z", k))
    cots = jnp.concatenate([cotangent, *cots], axis=0)
    cots, peaks = lax.optimization_barrier((cots, peaks))
    cots = [cots, swap(cots, "core")]
    rest1, rest2, *diagonal = lax.optimization_barrier((rest1, rest2, *diagonal))
    diagonal = jnp.concatenate(diagonal, axis=0)
    diagonal = [diagonal, swap(diagonal, "core")]
    slots = [
        ((r ^ dr) * 2 + (x ^ dx)) * 2 + (c ^ dc) for dc in (0, 1) for dr in (0, 1) for dx in (0, 1)
    ]
    slots = jnp.stack(slots).astype(jnp.int32)
    other = swap(for_other, "core")

    parts = [jnp.concatenate([own, peaks])]
    parts += [lax.dynamic_index_in_dim(mine, z ^ k, keepdims=False) for k in (1, 2, 3)]
    cots[1], *parts = lax.optimization_barrier((cots[1], *parts))
    side0 = swap(parts[0], "x")
    rest3 = swap(jnp.concatenate([parts[3], peaks]), "replica")
    swapped, other = lax.optimization_barrier((swapped, other))
    term = weight_terms(slots, swapped, cots + diagonal, (0, 1, 2, 3), [])
    stage = functools.partial(consume, where, scale, hidden, other, [cotangent, cots[1]])

    def codes_of(units):
        return [unit for _, _, unit in units]

    term, side0, rest3, *parts = lax.optimization_barrier((term, side0, rest3, *parts))
    rest3 = rest3[:half]
    total = lax.psum_scatter(term, "z", scatter_dimension=0, tiled=True)
    side1, other0 = swap(parts[1], "x"), swap(side0, "replica")
    units = [(own, 0, (0, 0, 0)), (rest0, 0, (0, 0, 1))] + [(mine, None, (k, 0, 0)) for k in (1, 2, 3)]
    *state, away0, away1 = stage(units, [], None)
    first = ([swap(away0, "core"), swap(away1, "core")], codes_of(units))

    peak = jnp.maximum(peaks, side0[half:])
    peak = jnp.max(jnp.maximum(peak, swap(peak, "core"))).astype(F32)
    peak_ratio = (peak / limit).reshape(1)

    parts[2], *state = lax.optimization_barrier((parts[2], *state))
    side2 = swap(parts[2], "x")
    side1, other0, peak_ratio, *state = lax.optimization_barrier((side1, other0, peak_ratio, *state))
    other1 = swap(side1, "replica")
    units = [(side0, 0, (0, 1, 0)), (other0, 0, (0, 1, 1)), (side1, 0, (1, 1, 0)), (rest1, 0, (1, 0, 1))]
    *state, away = stage(units, state, None)
    second = ([swap(away, "core")], codes_of(units))

    parts[3], *state = lax.optimization_barrier((parts[3], *state))
    side3 = swap(parts[3], "x")
    side2, other1, *state = lax.optimization_barrier((side2, other1, *state))
    other2 = swap(side2, "replica")
    units = [(rest2, 0, (2, 0, 1)), (rest3, 0, (3, 0, 1)), (other1, 0, (1, 1, 1)), (side2, 0, (2, 1, 0))]
    *state, away = stage(units, state, first)
    late, late_units = [swap(away, "core")], [codes_of(units)]

    rest3, *state = lax.optimization_barrier((rest3, *state))
    other3 = swap(rest3, "x")
    side3, other2, *state = lax.optimization_barrier((side3, other2, *state))
    units = [(other2, 0, (2, 1, 1)), (side3, 0, (3, 1, 0))]
    *state, away = stage(units, state, second, last=True)
    late.append(swap(away, "core"))
    late_units.append(codes_of(units))

    share = jnp.pad((total.astype(F32) * token_count ** (-0.5)).astype(BF16), ((0, 16), (0, 0)))
    other_share = swap(share, "replica")
    input_gradient, projected_keys = finish(
        where,
        scale,
        hidden,
        cotangent,
        (3, 1, 1),
        [other3, swap(other3, "core")],
        [state[0], swap(state[1], "core")],
        state[2],
        late,
        late_units,
    )
    weight_gradient = join(where, share, other_share)
    return (projected_keys, input_gradient, weight_gradient, peak_ratio)


def plain(hidden_states, key_weight, previous_peak, key_cotangent):
    names = ("replica", "x", "core")
    limit = previous_peak[0]
    unscale = limit / 448.0
    tokens, width = hidden_states.shape
    rows, features = key_weight.shape
    replicas = lax.axis_size("replica")
    nz, nx, nc = lax.axis_size("z"), lax.axis_size("x"), lax.axis_size("core")
    part = rows // replicas
    group = replicas * nx * nc
    split = hidden_states.reshape(tokens, nz, nx, nc, replicas, part)
    split = split.transpose(4, 2, 3, 0, 1, 5).reshape(group, tokens, nz * part)
    swapped = lax.all_to_all(split, names, 0, 0, tiled=True)
    cotangents = lax.all_gather(key_cotangent, names, axis=0, tiled=True)
    peak = lax.pmax(jnp.max(jnp.abs(key_weight.astype(F32))), ("z", "x", "core"))
    half = lax.dynamic_slice_in_dim(key_weight, lax.axis_index("replica") * part, part, 0)
    gathered = lax.all_gather(
        quantize(half, limit), ("z", "x", "core", "replica"), axis=0, tiled=True
    )
    keys_sum = jnp.dot(hidden_states, gathered, preferred_element_type=F32)
    grad_sum = lax.dot_general(
        key_cotangent, gathered, (((1,), (1,)), ((), ())), preferred_element_type=F32
    )
    term = lax.dot_general(
        swapped.reshape(group * tokens, nz * part),
        cotangents,
        (((0,), (0,)), ((), ())),
        preferred_element_type=F32,
    ).astype(BF16)
    total = lax.psum_scatter(term, "z", scatter_dimension=0, tiled=True).astype(F32)
    token_count = tokens * replicas * nz * nx * nc
    share = (total * token_count ** (-0.5)).astype(BF16)
    weight_gradient = lax.all_gather(share, "replica", axis=0, tiled=True)
    return (
        (keys_sum * unscale).astype(BF16),
        (grad_sum * unscale).astype(BF16),
        weight_gradient,
        (peak / limit).reshape(1),
    )


def solution(mesh):
    replicas, shards = mesh.shape["replica"], mesh.shape["fsdp"]
    grid = Mesh(mesh.devices.reshape(replicas, shards // 4, 2, 2), ("replica", "z", "x", "core"))
    fsdp = ("z", "x", "core")
    every = ("replica",) + fsdp
    in_specs = (P(every, None), P(fsdp, None), P(), P(every, None))
    out_specs = (P(every, None), P(every, None), P(fsdp, None), P())
    run = body if replicas == 2 and shards == 16 else plain
    return jax.shard_map(run, mesh=grid, in_specs=in_specs, out_specs=out_specs, check_vma=False)
```

```python
import functools

import jax
import jax.numpy as jnp
from jax import lax
from jax.experimental import pallas as pl
from jax.experimental.pallas import tpu as pltpu
from jax.sharding import Mesh
from jax.sharding import PartitionSpec as P

ANY = pl.BlockSpec(memory_space=pl.ANY)
SMEM = pl.BlockSpec(memory_space=pltpu.SMEM)
VMEM = pl.BlockSpec(memory_space=pltpu.VMEM)
PARAMS = pltpu.CompilerParams(vmem_limit_bytes=63 * 2**20)
CHEAP = pl.CostEstimate(flops=1, bytes_accessed=1, transcendentals=0)
F32, BF16 = jnp.float32, jnp.bfloat16


def quantize(weight, limit):
    return jnp.clip(weight.astype(F32) * (448.0 / limit), -448.0, 448.0).astype(BF16)


def swap(block, axis, mask=1):
    size = lax.axis_size(axis)
    return lax.ppermute(block, axis, [(i, i ^ mask) for i in range(size)])


def run(copies):
    for copy in copies:
        copy.start()
    for copy in copies:
        copy.wait()


def columns(start, size):
    return pl.ds(pl.multiple_of(start, size), size)


def pack(where, hidden, rows, nz):
    tokens = hidden.shape[0]
    half = rows // 2
    chips, blocks = ((0, 0), (0, 1), (1, 0), (1, 1)), nz * 2

    def kernel(where_ref, hidden_ref, *refs):
        group_refs, other_ref, sem = refs[:4], refs[4], refs[5]
        c, x, r = where_ref[0], where_ref[1], where_ref[2]
        copies = []
        for ref, (dr, dx) in zip(group_refs, chips):
            for dc in range(2):
                for k in range(nz):
                    start = (k * 4 + (x ^ dx) * 2 + (c ^ dc)) * rows + (r ^ dr) * half
                    copies.append(
                        pltpu.make_async_copy(
                            hidden_ref.at[:, columns(start, half)],
                            ref.at[dc, :, pl.ds(k * half, half)],
                            sem.at[len(copies)],
                        )
                    )
        for b in range(blocks):
            source = hidden_ref.at[:, columns((b * 2 + 1 - c) * rows, rows)]
            copies.append(pltpu.make_async_copy(source, other_ref.at[b], sem.at[len(copies)]))
        run(copies)

    return pl.pallas_call(
        kernel,
        out_shape=[jax.ShapeDtypeStruct((2, tokens, nz * half), BF16)] * 4
        + [jax.ShapeDtypeStruct((blocks, tokens, rows), BF16)],
        in_specs=[SMEM, ANY],
        out_specs=[VMEM] * 5,
        scratch_shapes=[pltpu.SemaphoreType.DMA((8 * nz + blocks,))],
        compiler_params=PARAMS,
        name="pack",
    )(where, hidden)


def weight_terms(sources, cotangents):
    tokens, width = sources[0].shape[1:]
    features = cotangents[0].shape[1]
    total, count = len(sources), 4
    tile = width // count

    def kernel(*refs):
        source_refs, cots_ref, refs = refs[:total], refs[total : total + 4], refs[total + 4 :]
        out_ref, lhs, rhs, out, sem, out_sem = refs
        copies = []
        for s in range(total):
            place = pl.ds(s * tokens, tokens)
            source = cots_ref[s // 4].at[pl.ds(s % 4 * tokens, tokens)] if s % 4 < 3 else cots_ref[2 + s // 4]
            copies.append(pltpu.make_async_copy(source, rhs.at[place], sem.at[count, s]))
        for i in range(count):
            at = pl.ds(i * tile, tile)
            for s in range(total):
                target = lhs.at[i, pl.ds(s * tokens, tokens)]
                copies.append(pltpu.make_async_copy(source_refs[s].at[s // 4, :, at], target, sem.at[i, s]))
        for copy in copies:
            copy.start()
        stores = []
        for i in range(count):
            for copy in copies[(i + 1 if i else 0) * total : (i + 2) * total]:
                copy.wait()
            out[i] = lax.dot_general(
                lhs[i], rhs[...], (((0,), (0,)), ((), ())), preferred_element_type=F32
            ).astype(BF16)
            target = out_ref.at[pl.ds(i * tile, tile)]
            stores.append(pltpu.make_async_copy(out.at[i], target, out_sem.at[i]))
            stores[-1].start()
        for copy in stores:
            copy.wait()

    return pl.pallas_call(
        kernel,
        out_shape=jax.ShapeDtypeStruct((width, features), BF16),
        in_specs=[ANY] * (total + 4),
        out_specs=ANY,
        scratch_shapes=[
            pltpu.VMEM((count, total * tokens, tile), BF16),
            pltpu.VMEM((total * tokens, features), BF16),
            pltpu.VMEM((count, tile, features), BF16),
            pltpu.SemaphoreType.DMA((count + 1, total)),
            pltpu.SemaphoreType.DMA((count,)),
        ],
        cost_estimate=CHEAP,
        compiler_params=PARAMS,
        name="weight_terms",
    )(*sources, *cotangents)


def consume(where, scale, hidden, other, cotangents, units, state, arrived, last=False):
    tokens, width = hidden.shape
    rows, features = other.shape[2], cotangents[0].shape[1]
    half = rows // 2
    count = len(units)
    extra = len(arrived[1]) if arrived else 0
    chunks = [min(4, count - i) for i in range(0, count, 4)]
    arrays = []
    for array, _, _ in units:
        if not any(array is known for known in arrays):
            arrays.append(array)

    def kernel(where_ref, scale_ref, hidden_ref, other_ref, *refs):
        cots_ref, refs = refs[:2], refs[2:]
        array_refs, refs = refs[: len(arrays)], refs[len(arrays) :]
        if state:
            totals_ref, refs = refs[:2], refs[3:]
        arrived_refs, refs = refs[: (extra + 3) // 4], refs[(extra + 3) // 4 :]
        total_refs, gradient_ref, away_refs, refs = refs[:2], refs[2], refs[3 : 3 + len(chunks)], refs[3 + len(chunks) :]
        hid, cot, wgt, acc, prior, near, far, held, sent, sem, cot_sem, out_sem, near_sem, far_sem = refs
        place = functools.partial(unit_columns, where_ref, rows)
        early = []
        for s in range(2):
            span = pl.ds(s * tokens, tokens)
            source = cots_ref[s].at[pl.ds(0, tokens)]
            early.append(pltpu.make_async_copy(source, cot.at[span], cot_sem.at[s]))
        for copy in early:
            copy.start()
        loads = []
        for b, (array, row, (k, side, part)) in enumerate(units):
            ref = [r for r, known in zip(array_refs, arrays) if known is array][0]
            at = pl.multiple_of((1 - where_ref[2] if part else where_ref[2]) * half, half)
            source = ref.at[where_ref[3] ^ k] if row is None else ref.at[pl.ds(row, half)]
            block = (where_ref[3] ^ k) * 2 + (1 - where_ref[1] if side else where_ref[1])
            pairs = [
                (source, wgt.at[b]),
                (hidden_ref.at[:, place((k, side, part), 0)], hid.at[b, pl.ds(0, tokens)]),
                (other_ref.at[block, :, pl.ds(at, half)], hid.at[b, pl.ds(tokens, tokens)]),
            ]
            loads.append([pltpu.make_async_copy(f, t, sem.at[i, b]) for i, (f, t) in enumerate(pairs)])
            for copy in loads[-1]:
                copy.start()
        before = []
        for i, ref in enumerate(arrived_refs):
            size = min(4, extra - 4 * i)
            before.append(pltpu.make_async_copy(ref, held.at[pl.ds(4 * i, size)], cot_sem.at[4 + i]))
        if state:
            for s in range(2):
                span = pl.ds(s * tokens, tokens)
                before.append(pltpu.make_async_copy(totals_ref[s], prior.at[span], cot_sem.at[2 + s]))
        for copy in before:
            copy.start()
        for copy in early:
            copy.wait()
        acc[...] = jnp.zeros_like(acc)

        def step(b, carry):
            for i, ref in enumerate((wgt.at[b], hid.at[b, pl.ds(0, tokens)], hid.at[b, pl.ds(0, tokens)])):
                pltpu.make_async_copy(ref, ref, sem.at[i, b]).wait()
            weight = wgt[b]
            acc[...] += jnp.dot(hid[b], weight, preferred_element_type=F32)
            product = (
                lax.dot_general(
                    cot[...], weight, (((1,), (1,)), ((), ())), preferred_element_type=F32
                )
                * scale_ref[0]
            ).astype(BF16)
            near[b] = product[:tokens]
            far[b] = product[tokens:]
            return carry

        lax.fori_loop(0, count, step, 0)
        late = [
            pltpu.make_async_copy(far.at[pl.ds(4 * i, size)], away_refs[i], far_sem.at[i])
            for i, size in enumerate(chunks)
        ]
        for b, (_, _, unit) in enumerate(units):
            late.append(
                pltpu.make_async_copy(near.at[b], gradient_ref.at[:, place(unit, 0)], near_sem.at[b])
            )
        for copy in late:
            copy.start()
        for copy in before:
            copy.wait()
        if state:
            acc[...] += prior[...]
        sums = [acc.at[pl.ds(s * tokens, tokens)] for s in range(2)]
        if last:
            sent[...] = acc[pl.ds(tokens, tokens)].astype(BF16)
            sums[1] = sent
        end = [pltpu.make_async_copy(sums[s], total_refs[s], out_sem.at[s]) for s in range(2)]
        for e in range(extra):
            columns = place(arrived[1][e], 1)
            end.append(
                pltpu.make_async_copy(held.at[e], gradient_ref.at[:, columns], out_sem.at[2 + e])
            )
        for copy in end:
            copy.start()
        for copy in late + end:
            copy.wait()

    sums = jax.ShapeDtypeStruct((tokens, features), F32)
    operands = [where, scale, hidden, other, *cotangents, *arrays, *state]
    if arrived:
        operands += arrived[0]
    return pl.pallas_call(
        kernel,
        out_shape=[
            sums,
            jax.ShapeDtypeStruct(sums.shape, BF16) if last else sums,
            jax.ShapeDtypeStruct((tokens, width), BF16),
            *[jax.ShapeDtypeStruct((size, tokens, half), BF16) for size in chunks],
        ],
        in_specs=[SMEM, SMEM] + [ANY] * (len(operands) - 2),
        out_specs=[ANY] * (3 + len(chunks)),
        input_output_aliases=(
            {6 + len(arrays) + i: i for i in (0, 2) + (() if last else (1,))} if state else {}
        ),
        scratch_shapes=[
            pltpu.VMEM((count, 2 * tokens, half), BF16),
            pltpu.VMEM((2 * tokens, features), BF16),
            pltpu.VMEM((count, half, features), BF16),
            pltpu.VMEM((2 * tokens, features), F32),
            pltpu.VMEM((2 * tokens, features) if state else (8, 128), F32),
            pltpu.VMEM((count, tokens, half), BF16),
            pltpu.VMEM((count, tokens, half), BF16),
            pltpu.VMEM((max(extra, 1), tokens, half), BF16),
            pltpu.VMEM((tokens, features) if last else (16, 128), BF16),
            pltpu.SemaphoreType.DMA((3, count)),
            pltpu.SemaphoreType.DMA((4 + (extra + 3) // 4,)),
            pltpu.SemaphoreType.DMA((2 + extra,)),
            pltpu.SemaphoreType.DMA((count,)),
            pltpu.SemaphoreType.DMA((len(chunks),)),
        ],
        cost_estimate=CHEAP,
        compiler_params=PARAMS,
        name="consume",
    )(*operands)


def unit_columns(where_ref, rows, unit, core):
    k, side, part = unit
    half = rows // 2
    x = 1 - where_ref[1] if side else where_ref[1]
    c = 1 - where_ref[0] if core else where_ref[0]
    r = 1 - where_ref[2] if part else where_ref[2]
    at = (((where_ref[3] ^ k) * 2 + x) * 2 + c) * rows + r * half
    return pl.ds(pl.multiple_of(at, half), half)


def finish(where, scale, hidden, cotangent, unit, weights, sums, gradient, arrived, units):
    tokens, width = hidden.shape
    half, features = weights[0].shape
    counts = [len(some) for some in units]

    def kernel(where_ref, scale_ref, hidden_ref, cot_ref, *refs):
        weight_refs, sum_refs, arrived_refs, refs = refs[:2], refs[2:4], refs[4 : 4 + len(units)], refs[5 + len(units) :]
        gradient_ref, keys_ref, hid, cot, wgt, near, far, held, new, sem, held_sem, out_sem = refs
        place = functools.partial(unit_columns, where_ref, 2 * half)
        loads = [pltpu.make_async_copy(cot_ref, cot, sem.at[0])]
        for i in range(2):
            loads.append(pltpu.make_async_copy(weight_refs[i], wgt.at[i], sem.at[1 + i]))
            columns = hidden_ref.at[:, place(unit, i)]
            loads.append(pltpu.make_async_copy(columns, hid.at[i], sem.at[3 + i]))
        loads.append(pltpu.make_async_copy(sum_refs[0], near, sem.at[5]))
        loads.append(pltpu.make_async_copy(sum_refs[1], far, sem.at[6]))
        for copy in loads:
            copy.start()
        fills, stores = [], []
        for j, (ref, some) in enumerate(zip(arrived_refs, units)):
            first = sum(counts[:j])
            fills.append(pltpu.make_async_copy(ref, held.at[pl.ds(first, len(some))], held_sem.at[j]))
            fills[-1].start()
            for e, one in enumerate(some):
                target = gradient_ref.at[:, place(one, 1)]
                stores.append(pltpu.make_async_copy(held.at[first + e], target, out_sem.at[2 + first + e]))
        for copy in loads[:5]:
            copy.wait()
        for i in range(2):
            new[i] = (
                lax.dot_general(
                    cot[...], wgt[i], (((1,), (1,)), ((), ())), preferred_element_type=F32
                )
                * scale_ref[0]
            ).astype(BF16)
            target = gradient_ref.at[:, place(unit, i)]
            stores.append(pltpu.make_async_copy(new.at[i], target, out_sem.at[i]))
            stores[-1].start()
        for copy in fills:
            copy.wait()
        for copy in stores[:-2]:
            copy.start()
        total = jnp.dot(hid[0], wgt[0], preferred_element_type=F32)
        total += jnp.dot(hid[1], wgt[1], preferred_element_type=F32)
        for copy in loads[5:]:
            copy.wait()
        keys_ref[...] = ((total + near[...] + far[...].astype(F32)) * scale_ref[0]).astype(BF16)
        for copy in stores:
            copy.wait()

    return pl.pallas_call(
        kernel,
        out_shape=[
            jax.ShapeDtypeStruct(gradient.shape, BF16),
            jax.ShapeDtypeStruct((tokens, features), BF16),
        ],
        in_specs=[SMEM, SMEM] + [ANY] * (7 + len(units)),
        out_specs=[ANY, VMEM],
        input_output_aliases={8 + len(units): 0},
        scratch_shapes=[
            pltpu.VMEM((2, tokens, half), BF16),
            pltpu.VMEM((tokens, features), BF16),
            pltpu.VMEM((2, half, features), BF16),
            pltpu.VMEM((tokens, features), F32),
            pltpu.VMEM((tokens, features), BF16),
            pltpu.VMEM((sum(counts), tokens, half), BF16),
            pltpu.VMEM((2, tokens, half), BF16),
            pltpu.SemaphoreType.DMA((7,)),
            pltpu.SemaphoreType.DMA((len(units),)),
            pltpu.SemaphoreType.DMA((2 + sum(counts),)),
        ],
        cost_estimate=CHEAP,
        compiler_params=PARAMS,
        name="finish",
    )(where, scale, hidden, cotangent, *weights, *sums, *arrived, gradient)


def join(where, mine, theirs):
    half, features = mine.shape[0] - 16, mine.shape[1]

    def kernel(where_ref, mine_ref, theirs_ref, out_ref):
        at = pl.multiple_of(where_ref[2] * half, half)
        out_ref[pl.ds(at, half), :] = mine_ref[pl.ds(0, half), :]
        out_ref[pl.ds(half - at, half), :] = theirs_ref[pl.ds(0, half), :]

    return pl.pallas_call(
        kernel,
        out_shape=jax.ShapeDtypeStruct((2 * half, features), BF16),
        in_specs=[SMEM, VMEM, VMEM],
        out_specs=VMEM,
        compiler_params=PARAMS,
        name="join",
    )(where, mine, theirs)


def body(hidden, key_weight, previous_peak, cotangent):
    limit = previous_peak[0]
    unscale = limit / 448.0
    scale = unscale.reshape(1)
    tokens = hidden.shape[0]
    rows = key_weight.shape[0]
    r, z, x, c = (lax.axis_index(name) for name in ("replica", "z", "x", "core"))
    where = jnp.stack([c, x, r, z]).astype(jnp.int32)
    nz = lax.axis_size("z")
    token_count = tokens * lax.axis_size(("replica", "z", "x", "core"))

    half = rows // 2
    own = quantize(lax.dynamic_slice_in_dim(key_weight, r * half, half, 0), limit)
    rest = quantize(lax.dynamic_slice_in_dim(key_weight, (1 - r) * half, half, 0), limit)
    hidden, own, rest = lax.optimization_barrier((hidden, own, rest))
    mine = lax.all_gather(own, "z", axis=0)
    rest0, mine = lax.optimization_barrier((rest, mine))
    rest1, rest2 = swap(rest0, "z", 1), swap(rest0, "z", 2)

    cots = [swap(cotangent, "x"), swap(cotangent, "replica")]
    here, for_x, for_y, for_xy, for_other = pack(where, hidden, rows, nz)
    for_xy, for_y, *cots = lax.optimization_barrier((for_xy, for_y, *cots))
    via_x, from_y = swap(for_xy, "x"), swap(for_y, "replica")
    via_x, from_y, for_x = lax.optimization_barrier((via_x, from_y, for_x))
    from_x, from_xy = swap(for_x, "x"), swap(via_x, "replica")
    cut = tokens // 2
    after_x, after_y, rest1 = lax.optimization_barrier((cots[0], cots[1], rest1))
    diagonal = [swap(after_y[:cut], "x"), swap(after_x[cut:], "replica")]
    peaks = jnp.max(jnp.abs(key_weight), axis=0, keepdims=True)
    peaks = jnp.broadcast_to(peaks, (16, peaks.shape[1]))
    for k in (1, 2):
        peaks = jnp.maximum(peaks, swap(peaks, "z", k))
    cots = jnp.concatenate([cotangent, *cots], axis=0)
    cots, peaks = lax.optimization_barrier((cots, peaks))
    cots = [cots, swap(cots, "core")]
    rest1, rest2, *diagonal = lax.optimization_barrier((rest1, rest2, *diagonal))
    diagonal = jnp.concatenate(diagonal, axis=0)
    diagonal = [diagonal, swap(diagonal, "core")]
    other = swap(for_other, "core")

    parts = [jnp.concatenate([own, peaks])]
    parts += [lax.dynamic_index_in_dim(mine, z ^ k, keepdims=False) for k in (1, 2, 3)]
    cots[1], *parts = lax.optimization_barrier((cots[1], *parts))
    side0 = swap(parts[0], "x")
    rest3 = swap(jnp.concatenate([parts[3], peaks]), "replica")
    sources = [here, from_x, from_y, from_xy]
    sources += [swap(source, "core") for source in sources]
    other, *sources = lax.optimization_barrier((other, *sources))
    term = weight_terms(sources, cots + diagonal)
    stage = functools.partial(consume, where, scale, hidden, other, [cotangent, cots[1]])

    def codes_of(units):
        return [unit for _, _, unit in units]

    term, side0, rest3, *parts = lax.optimization_barrier((term, side0, rest3, *parts))
    rest3 = rest3[:half]
    total = lax.psum_scatter(term, "z", scatter_dimension=0, tiled=True)
    side1, other0 = swap(parts[1], "x"), swap(side0, "replica")
    units = [(own, 0, (0, 0, 0)), (rest0, 0, (0, 0, 1))] + [(mine, None, (k, 0, 0)) for k in (1, 2, 3)]
    *state, away0, away1 = stage(units, [], None)
    first = ([swap(away0, "core"), swap(away1, "core")], codes_of(units))

    peak = jnp.maximum(peaks, side0[half:])
    peak = jnp.max(jnp.maximum(peak, swap(peak, "core"))).astype(F32)
    peak_ratio = (peak / limit).reshape(1)

    parts[2], *state = lax.optimization_barrier((parts[2], *state))
    side2 = swap(parts[2], "x")
    side1, other0, peak_ratio, *state = lax.optimization_barrier((side1, other0, peak_ratio, *state))
    other1 = swap(side1, "replica")
    units = [(side0, 0, (0, 1, 0)), (other0, 0, (0, 1, 1)), (side1, 0, (1, 1, 0)), (rest1, 0, (1, 0, 1))]
    *state, away = stage(units, state, None)
    second = ([swap(away, "core")], codes_of(units))

    parts[3], *state = lax.optimization_barrier((parts[3], *state))
    side3 = swap(parts[3], "x")
    side2, other1, *state = lax.optimization_barrier((side2, other1, *state))
    other2 = swap(side2, "replica")
    units = [(rest2, 0, (2, 0, 1)), (rest3, 0, (3, 0, 1)), (other1, 0, (1, 1, 1)), (side2, 0, (2, 1, 0))]
    *state, away = stage(units, state, first)
    late, late_units = [swap(away, "core")], [codes_of(units)]

    rest3, *state = lax.optimization_barrier((rest3, *state))
    other3 = swap(rest3, "x")
    side3, other2, *state = lax.optimization_barrier((side3, other2, *state))
    units = [(other2, 0, (2, 1, 1)), (side3, 0, (3, 1, 0))]
    *state, away = stage(units, state, second, last=True)
    late.append(swap(away, "core"))
    late_units.append(codes_of(units))

    share = jnp.pad((total.astype(F32) * token_count ** (-0.5)).astype(BF16), ((0, 16), (0, 0)))
    other_share = swap(share, "replica")
    input_gradient, projected_keys = finish(
        where,
        scale,
        hidden,
        cotangent,
        (3, 1, 1),
        [other3, swap(other3, "core")],
        [state[0], swap(state[1], "core")],
        state[2],
        late,
        late_units,
    )
    weight_gradient = join(where, share, other_share)
    return (projected_keys, input_gradient, weight_gradient, peak_ratio)


def plain(hidden_states, key_weight, previous_peak, key_cotangent):
    names = ("replica", "x", "core")
    limit = previous_peak[0]
    unscale = limit / 448.0
    tokens, width = hidden_states.shape
    rows, features = key_weight.shape
    replicas = lax.axis_size("replica")
    nz, nx, nc = lax.axis_size("z"), lax.axis_size("x"), lax.axis_size("core")
    part = rows // replicas
    group = replicas * nx * nc
    split = hidden_states.reshape(tokens, nz, nx, nc, replicas, part)
    split = split.transpose(4, 2, 3, 0, 1, 5).reshape(group, tokens, nz * part)
    swapped = lax.all_to_all(split, names, 0, 0, tiled=True)
    cotangents = lax.all_gather(key_cotangent, names, axis=0, tiled=True)
    peak = lax.pmax(jnp.max(jnp.abs(key_weight.astype(F32))), ("z", "x", "core"))
    half = lax.dynamic_slice_in_dim(key_weight, lax.axis_index("replica") * part, part, 0)
    gathered = lax.all_gather(
        quantize(half, limit), ("z", "x", "core", "replica"), axis=0, tiled=True
    )
    keys_sum = jnp.dot(hidden_states, gathered, preferred_element_type=F32)
    grad_sum = lax.dot_general(
        key_cotangent, gathered, (((1,), (1,)), ((), ())), preferred_element_type=F32
    )
    term = lax.dot_general(
        swapped.reshape(group * tokens, nz * part),
        cotangents,
        (((0,), (0,)), ((), ())),
        preferred_element_type=F32,
    ).astype(BF16)
    total = lax.psum_scatter(term, "z", scatter_dimension=0, tiled=True).astype(F32)
    token_count = tokens * replicas * nz * nx * nc
    share = (total * token_count ** (-0.5)).astype(BF16)
    weight_gradient = lax.all_gather(share, "replica", axis=0, tiled=True)
    return (
        (keys_sum * unscale).astype(BF16),
        (grad_sum * unscale).astype(BF16),
        weight_gradient,
        (peak / limit).reshape(1),
    )


def solution(mesh):
    replicas, shards = mesh.shape["replica"], mesh.shape["fsdp"]
    grid = Mesh(mesh.devices.reshape(replicas, shards // 4, 2, 2), ("replica", "z", "x", "core"))
    fsdp = ("z", "x", "core")
    every = ("replica",) + fsdp
    in_specs = (P(every, None), P(fsdp, None), P(), P(every, None))
    out_specs = (P(every, None), P(every, None), P(fsdp, None), P())
    run = body if replicas == 2 and shards == 16 else plain
    return jax.shard_map(run, mesh=grid, in_specs=in_specs, out_specs=out_specs, check_vma=False)
```

```python
import functools

import jax
import jax.numpy as jnp
from jax import lax
from jax.experimental import pallas as pl
from jax.experimental.pallas import tpu as pltpu
from jax.sharding import Mesh
from jax.sharding import PartitionSpec as P

ANY = pl.BlockSpec(memory_space=pl.ANY)
SMEM = pl.BlockSpec(memory_space=pltpu.SMEM)
VMEM = pl.BlockSpec(memory_space=pltpu.VMEM)
PARAMS = pltpu.CompilerParams(vmem_limit_bytes=63 * 2**20)
CHEAP = pl.CostEstimate(flops=1, bytes_accessed=1, transcendentals=0)
F32, BF16 = jnp.float32, jnp.bfloat16


def quantize(weight, limit):
    return jnp.clip(weight.astype(F32) * (448.0 / limit), -448.0, 448.0).astype(BF16)


def swap(block, axis, mask=1):
    size = lax.axis_size(axis)
    return lax.ppermute(block, axis, [(i, i ^ mask) for i in range(size)])


def run(copies):
    for copy in copies:
        copy.start()
    for copy in copies:
        copy.wait()


def pack(core, hidden, rows, nz):
    tokens = hidden.shape[0]
    half = rows // 2
    group, blocks = 8, nz * 2

    def kernel(core_ref, hidden_ref, group_ref, other_ref, sem):
        copies = []
        for d in range(group):
            for k in range(nz):
                start = (k * 4 + d % 4) * rows + (d // 4) * half
                copies.append(
                    pltpu.make_async_copy(
                        hidden_ref.at[:, pl.ds(start, half)],
                        group_ref.at[d, :, pl.ds(k * half, half)],
                        sem.at[len(copies)],
                    )
                )
        for b in range(blocks):
            start = pl.multiple_of((b * 2 + 1 - core_ref[0]) * rows, rows)
            copies.append(
                pltpu.make_async_copy(
                    hidden_ref.at[:, pl.ds(start, rows)], other_ref.at[b], sem.at[len(copies)]
                )
            )
        run(copies)

    return pl.pallas_call(
        kernel,
        out_shape=[
            jax.ShapeDtypeStruct((group, tokens, nz * half), BF16),
            jax.ShapeDtypeStruct((blocks, tokens, rows), BF16),
        ],
        in_specs=[SMEM, ANY],
        out_specs=[VMEM, VMEM],
        scratch_shapes=[pltpu.SemaphoreType.DMA((group * nz + blocks,))],
        compiler_params=PARAMS,
        name="pack",
    )(core, hidden)


def weight_terms(slots, swapped, cotangents, tiles, state):
    sources, tokens, width = swapped.shape
    features = cotangents[0].shape[1]
    count = len(tiles)
    tile = width // 4

    def kernel(slots_ref, swapped_ref, *refs):
        cots_ref, refs = refs[:4], refs[4 + len(state) :]
        out_ref, lhs, rhs, out, sem, out_sem = refs
        copies = []
        for s in range(sources):
            place = pl.ds(pl.multiple_of(slots_ref[s] * tokens, tokens), tokens)
            source = cots_ref[s // 4].at[pl.ds(s % 4 * tokens, tokens)] if s % 4 < 3 else cots_ref[2 + s // 4]
            copies.append(pltpu.make_async_copy(source, rhs.at[place], sem.at[count, s]))
        for i, t in enumerate(tiles):
            at = pl.ds(t * tile, tile)
            for s in range(sources):
                place = pl.ds(s * tokens, tokens)
                copies.append(
                    pltpu.make_async_copy(swapped_ref.at[s, :, at], lhs.at[i, place], sem.at[i, s])
                )
        for copy in copies:
            copy.start()
        stores = []
        for i, t in enumerate(tiles):
            for copy in copies[(i + 1 if i else 0) * sources : (i + 2) * sources]:
                copy.wait()
            out[i] = lax.dot_general(
                lhs[i], rhs[...], (((0,), (0,)), ((), ())), preferred_element_type=F32
            ).astype(BF16)
            target = out_ref.at[pl.ds(t * tile, tile)]
            stores.append(pltpu.make_async_copy(out.at[i], target, out_sem.at[i]))
            stores[-1].start()
        for copy in stores:
            copy.wait()

    return pl.pallas_call(
        kernel,
        out_shape=jax.ShapeDtypeStruct((width, features), BF16),
        in_specs=[SMEM] + [ANY] * (5 + len(state)),
        out_specs=ANY,
        input_output_aliases={6: 0} if state else {},
        scratch_shapes=[
            pltpu.VMEM((count, sources * tokens, tile), BF16),
            pltpu.VMEM((sources * tokens, features), BF16),
            pltpu.VMEM((count, tile, features), BF16),
            pltpu.SemaphoreType.DMA((count + 1, sources)),
            pltpu.SemaphoreType.DMA((count,)),
        ],
        cost_estimate=CHEAP,
        compiler_params=PARAMS,
        name="weight_terms",
    )(slots, swapped, *cotangents, *state)


def consume(where, scale, hidden, other, cotangents, units, state, arrived, last=False):
    tokens, width = hidden.shape
    rows, features = other.shape[2], cotangents[0].shape[1]
    half = rows // 2
    count = len(units)
    extra = len(arrived[1]) if arrived else 0
    chunks = [min(4, count - i) for i in range(0, count, 4)]
    arrays = []
    for array, _, _ in units:
        if not any(array is known for known in arrays):
            arrays.append(array)

    def kernel(where_ref, scale_ref, hidden_ref, other_ref, *refs):
        cots_ref, refs = refs[:2], refs[2:]
        array_refs, refs = refs[: len(arrays)], refs[len(arrays) :]
        if state:
            totals_ref, refs = refs[:2], refs[3:]
        arrived_refs, refs = refs[: (extra + 3) // 4], refs[(extra + 3) // 4 :]
        total_refs, gradient_ref, away_refs, refs = refs[:2], refs[2], refs[3 : 3 + len(chunks)], refs[3 + len(chunks) :]
        hid, cot, wgt, acc, prior, near, far, held, sent, sem, cot_sem, out_sem, near_sem, far_sem = refs
        place = functools.partial(unit_columns, where_ref, rows)
        early = []
        for s in range(2):
            span = pl.ds(s * tokens, tokens)
            source = cots_ref[s].at[pl.ds(0, tokens)]
            early.append(pltpu.make_async_copy(source, cot.at[span], cot_sem.at[s]))
        for copy in early:
            copy.start()
        loads = []
        for b, (array, row, (k, side, part)) in enumerate(units):
            ref = [r for r, known in zip(array_refs, arrays) if known is array][0]
            at = pl.multiple_of((1 - where_ref[2] if part else where_ref[2]) * half, half)
            source = ref.at[where_ref[3] ^ k] if row is None else ref.at[pl.ds(row, half)]
            block = (where_ref[3] ^ k) * 2 + (1 - where_ref[1] if side else where_ref[1])
            pairs = [
                (source, wgt.at[b]),
                (hidden_ref.at[:, place((k, side, part), 0)], hid.at[b, pl.ds(0, tokens)]),
                (other_ref.at[block, :, pl.ds(at, half)], hid.at[b, pl.ds(tokens, tokens)]),
            ]
            loads.append([pltpu.make_async_copy(f, t, sem.at[i, b]) for i, (f, t) in enumerate(pairs)])
            for copy in loads[-1]:
                copy.start()
        before = []
        for i, ref in enumerate(arrived_refs):
            size = min(4, extra - 4 * i)
            before.append(pltpu.make_async_copy(ref, held.at[pl.ds(4 * i, size)], cot_sem.at[4 + i]))
        if state:
            for s in range(2):
                span = pl.ds(s * tokens, tokens)
                before.append(pltpu.make_async_copy(totals_ref[s], prior.at[span], cot_sem.at[2 + s]))
        for copy in before:
            copy.start()
        for copy in early:
            copy.wait()
        acc[...] = jnp.zeros_like(acc)

        def step(b, carry):
            for i, ref in enumerate((wgt.at[b], hid.at[b, pl.ds(0, tokens)], hid.at[b, pl.ds(0, tokens)])):
                pltpu.make_async_copy(ref, ref, sem.at[i, b]).wait()
            weight = wgt[b]
            acc[...] += jnp.dot(hid[b], weight, preferred_element_type=F32)
            product = (
                lax.dot_general(
                    cot[...], weight, (((1,), (1,)), ((), ())), preferred_element_type=F32
                )
                * scale_ref[0]
            ).astype(BF16)
            near[b] = product[:tokens]
            far[b] = product[tokens:]
            return carry

        lax.fori_loop(0, count, step, 0)
        late = [
            pltpu.make_async_copy(far.at[pl.ds(4 * i, size)], away_refs[i], far_sem.at[i])
            for i, size in enumerate(chunks)
        ]
        for b, (_, _, unit) in enumerate(units):
            late.append(
                pltpu.make_async_copy(near.at[b], gradient_ref.at[:, place(unit, 0)], near_sem.at[b])
            )
        for copy in late:
            copy.start()
        for copy in before:
            copy.wait()
        if state:
            acc[...] += prior[...]
        sums = [acc.at[pl.ds(s * tokens, tokens)] for s in range(2)]
        if last:
            sent[...] = acc[pl.ds(tokens, tokens)].astype(BF16)
            sums[1] = sent
        end = [pltpu.make_async_copy(sums[s], total_refs[s], out_sem.at[s]) for s in range(2)]
        for e in range(extra):
            columns = place(arrived[1][e], 1)
            end.append(
                pltpu.make_async_copy(held.at[e], gradient_ref.at[:, columns], out_sem.at[2 + e])
            )
        for copy in end:
            copy.start()
        for copy in late + end:
            copy.wait()

    sums = jax.ShapeDtypeStruct((tokens, features), F32)
    operands = [where, scale, hidden, other, *cotangents, *arrays, *state]
    if arrived:
        operands += arrived[0]
    return pl.pallas_call(
        kernel,
        out_shape=[
            sums,
            jax.ShapeDtypeStruct(sums.shape, BF16) if last else sums,
            jax.ShapeDtypeStruct((tokens, width), BF16),
            *[jax.ShapeDtypeStruct((size, tokens, half), BF16) for size in chunks],
        ],
        in_specs=[SMEM, SMEM] + [ANY] * (len(operands) - 2),
        out_specs=[ANY] * (3 + len(chunks)),
        input_output_aliases=(
            {6 + len(arrays) + i: i for i in (0, 2) + (() if last else (1,))} if state else {}
        ),
        scratch_shapes=[
            pltpu.VMEM((count, 2 * tokens, half), BF16),
            pltpu.VMEM((2 * tokens, features), BF16),
            pltpu.VMEM((count, half, features), BF16),
            pltpu.VMEM((2 * tokens, features), F32),
            pltpu.VMEM((2 * tokens, features) if state else (8, 128), F32),
            pltpu.VMEM((count, tokens, half), BF16),
            pltpu.VMEM((count, tokens, half), BF16),
            pltpu.VMEM((max(extra, 1), tokens, half), BF16),
            pltpu.VMEM((tokens, features) if last else (16, 128), BF16),
            pltpu.SemaphoreType.DMA((3, count)),
            pltpu.SemaphoreType.DMA((4 + (extra + 3) // 4,)),
            pltpu.SemaphoreType.DMA((2 + extra,)),
            pltpu.SemaphoreType.DMA((count,)),
            pltpu.SemaphoreType.DMA((len(chunks),)),
        ],
        cost_estimate=CHEAP,
        compiler_params=PARAMS,
        name="consume",
    )(*operands)


def unit_columns(where_ref, rows, unit, core):
    k, side, part = unit
    half = rows // 2
    x = 1 - where_ref[1] if side else where_ref[1]
    c = 1 - where_ref[0] if core else where_ref[0]
    r = 1 - where_ref[2] if part else where_ref[2]
    at = (((where_ref[3] ^ k) * 2 + x) * 2 + c) * rows + r * half
    return pl.ds(pl.multiple_of(at, half), half)


def finish(where, scale, hidden, cotangent, unit, weights, sums, gradient, arrived, units):
    tokens, width = hidden.shape
    half, features = weights[0].shape
    counts = [len(some) for some in units]

    def kernel(where_ref, scale_ref, hidden_ref, cot_ref, *refs):
        weight_refs, sum_refs, arrived_refs, refs = refs[:2], refs[2:4], refs[4 : 4 + len(units)], refs[5 + len(units) :]
        gradient_ref, keys_ref, hid, cot, wgt, near, far, held, new, sem, held_sem, out_sem = refs
        place = functools.partial(unit_columns, where_ref, 2 * half)
        loads = [pltpu.make_async_copy(cot_ref, cot, sem.at[0])]
        for i in range(2):
            loads.append(pltpu.make_async_copy(weight_refs[i], wgt.at[i], sem.at[1 + i]))
            columns = hidden_ref.at[:, place(unit, i)]
            loads.append(pltpu.make_async_copy(columns, hid.at[i], sem.at[3 + i]))
        loads.append(pltpu.make_async_copy(sum_refs[0], near, sem.at[5]))
        loads.append(pltpu.make_async_copy(sum_refs[1], far, sem.at[6]))
        for copy in loads:
            copy.start()
        fills, stores = [], []
        for j, (ref, some) in enumerate(zip(arrived_refs, units)):
            first = sum(counts[:j])
            fills.append(pltpu.make_async_copy(ref, held.at[pl.ds(first, len(some))], held_sem.at[j]))
            fills[-1].start()
            for e, one in enumerate(some):
                target = gradient_ref.at[:, place(one, 1)]
                stores.append(pltpu.make_async_copy(held.at[first + e], target, out_sem.at[2 + first + e]))
        for copy in loads[:5]:
            copy.wait()
        for i in range(2):
            new[i] = (
                lax.dot_general(
                    cot[...], wgt[i], (((1,), (1,)), ((), ())), preferred_element_type=F32
                )
                * scale_ref[0]
            ).astype(BF16)
            target = gradient_ref.at[:, place(unit, i)]
            stores.append(pltpu.make_async_copy(new.at[i], target, out_sem.at[i]))
            stores[-1].start()
        for copy in fills:
            copy.wait()
        for copy in stores[:-2]:
            copy.start()
        total = jnp.dot(hid[0], wgt[0], preferred_element_type=F32)
        total += jnp.dot(hid[1], wgt[1], preferred_element_type=F32)
        for copy in loads[5:]:
            copy.wait()
        keys_ref[...] = ((total + near[...] + far[...].astype(F32)) * scale_ref[0]).astype(BF16)
        for copy in stores:
            copy.wait()

    return pl.pallas_call(
        kernel,
        out_shape=[
            jax.ShapeDtypeStruct(gradient.shape, BF16),
            jax.ShapeDtypeStruct((tokens, features), BF16),
        ],
        in_specs=[SMEM, SMEM] + [ANY] * (7 + len(units)),
        out_specs=[ANY, VMEM],
        input_output_aliases={8 + len(units): 0},
        scratch_shapes=[
            pltpu.VMEM((2, tokens, half), BF16),
            pltpu.VMEM((tokens, features), BF16),
            pltpu.VMEM((2, half, features), BF16),
            pltpu.VMEM((tokens, features), F32),
            pltpu.VMEM((tokens, features), BF16),
            pltpu.VMEM((sum(counts), tokens, half), BF16),
            pltpu.VMEM((2, tokens, half), BF16),
            pltpu.SemaphoreType.DMA((7,)),
            pltpu.SemaphoreType.DMA((len(units),)),
            pltpu.SemaphoreType.DMA((2 + sum(counts),)),
        ],
        cost_estimate=CHEAP,
        compiler_params=PARAMS,
        name="finish",
    )(where, scale, hidden, cotangent, *weights, *sums, *arrived, gradient)


def join(where, mine, theirs):
    half, features = mine.shape[0] - 16, mine.shape[1]

    def kernel(where_ref, mine_ref, theirs_ref, out_ref):
        at = pl.multiple_of(where_ref[2] * half, half)
        out_ref[pl.ds(at, half), :] = mine_ref[pl.ds(0, half), :]
        out_ref[pl.ds(half - at, half), :] = theirs_ref[pl.ds(0, half), :]

    return pl.pallas_call(
        kernel,
        out_shape=jax.ShapeDtypeStruct((2 * half, features), BF16),
        in_specs=[SMEM, VMEM, VMEM],
        out_specs=VMEM,
        compiler_params=PARAMS,
        name="join",
    )(where, mine, theirs)


def body(hidden, key_weight, previous_peak, cotangent):
    limit = previous_peak[0]
    unscale = limit / 448.0
    scale = unscale.reshape(1)
    tokens = hidden.shape[0]
    rows = key_weight.shape[0]
    r, z, x, c = (lax.axis_index(name) for name in ("replica", "z", "x", "core"))
    where = jnp.stack([c, x, r, z]).astype(jnp.int32)
    nz = lax.axis_size("z")
    token_count = tokens * lax.axis_size(("replica", "z", "x", "core"))

    half = rows // 2
    own = quantize(lax.dynamic_slice_in_dim(key_weight, r * half, half, 0), limit)
    rest = quantize(lax.dynamic_slice_in_dim(key_weight, (1 - r) * half, half, 0), limit)
    hidden, own, rest = lax.optimization_barrier((hidden, own, rest))
    mine = lax.all_gather(own, "z", axis=0)
    rest0, mine = lax.optimization_barrier((rest, mine))
    rest1, rest2 = swap(rest0, "z", 1), swap(rest0, "z", 2)

    cots = [swap(cotangent, "x"), swap(cotangent, "replica")]
    for_group, for_other = pack(where, hidden, rows, nz)
    for_group, *cots = lax.optimization_barrier((for_group, *cots))
    swapped = lax.all_to_all(for_group, ("replica", "x", "core"), 0, 0, tiled=True)
    cut = tokens // 2
    diagonal = [swap(cots[1][:cut], "x"), swap(cots[0][cut:], "replica")]
    peaks = jnp.max(jnp.abs(key_weight), axis=0, keepdims=True)
    peaks = jnp.broadcast_to(peaks, (16, peaks.shape[1]))
    for k in (1, 2):
        peaks = jnp.maximum(peaks, swap(peaks, "z", k))
    cots = jnp.concatenate([cotangent, *cots], axis=0)
    cots, peaks = lax.optimization_barrier((cots, peaks))
    cots = [cots, swap(cots, "core")]
    rest1, rest2, *diagonal = lax.optimization_barrier((rest1, rest2, *diagonal))
    diagonal = jnp.concatenate(diagonal, axis=0)
    diagonal = [diagonal, swap(diagonal, "core")]
    slots = [
        ((r ^ dr) * 2 + (x ^ dx)) * 2 + (c ^ dc) for dc in (0, 1) for dr in (0, 1) for dx in (0, 1)
    ]
    slots = jnp.stack(slots).astype(jnp.int32)
    other = swap(for_other, "core")

    parts = [jnp.concatenate([own, peaks])]
    parts += [lax.dynamic_index_in_dim(mine, z ^ k, keepdims=False) for k in (1, 2, 3)]
    cots[1], *parts = lax.optimization_barrier((cots[1], *parts))
    side0 = swap(parts[0], "x")
    rest3 = swap(jnp.concatenate([parts[3], peaks]), "replica")
    swapped, other = lax.optimization_barrier((swapped, other))
    term = weight_terms(slots, swapped, cots + diagonal, (0, 1, 2, 3), [])
    stage = functools.partial(consume, where, scale, hidden, other, [cotangent, cots[1]])

    def codes_of(units):
        return [unit for _, _, unit in units]

    term, side0, rest3, *parts = lax.optimization_barrier((term, side0, rest3, *parts))
    rest3 = rest3[:half]
    total = lax.psum_scatter(term, "z", scatter_dimension=0, tiled=True)
    side1, other0 = swap(parts[1], "x"), swap(side0, "replica")
    units = [(own, 0, (0, 0, 0)), (rest0, 0, (0, 0, 1))] + [(mine, None, (k, 0, 0)) for k in (1, 2, 3)]
    *state, away0, away1 = stage(units, [], None)
    first = ([swap(away0, "core"), swap(away1, "core")], codes_of(units))

    peak = jnp.maximum(peaks, side0[half:])
    peak = jnp.max(jnp.maximum(peak, swap(peak, "core"))).astype(F32)
    peak_ratio = (peak / limit).reshape(1)

    parts[2], *state = lax.optimization_barrier((parts[2], *state))
    side2 = swap(parts[2], "x")
    side1, other0, peak_ratio, *state = lax.optimization_barrier((side1, other0, peak_ratio, *state))
    other1 = swap(side1, "replica")
    units = [(side0, 0, (0, 1, 0)), (other0, 0, (0, 1, 1)), (side1, 0, (1, 1, 0)), (rest1, 0, (1, 0, 1))]
    *state, away = stage(units, state, None)
    second = ([swap(away, "core")], codes_of(units))

    parts[3], *state = lax.optimization_barrier((parts[3], *state))
    side3 = swap(parts[3], "x")
    side2, other1, *state = lax.optimization_barrier((side2, other1, *state))
    other2 = swap(side2, "replica")
    units = [(rest2, 0, (2, 0, 1)), (rest3, 0, (3, 0, 1)), (other1, 0, (1, 1, 1)), (side2, 0, (2, 1, 0))]
    *state, away = stage(units, state, first)
    late, late_units = [swap(away, "core")], [codes_of(units)]

    rest3, *state = lax.optimization_barrier((rest3, *state))
    other3 = swap(rest3, "x")
    units = [(side3, 0, (3, 1, 0))]
    *state, away = stage(units, state, second)
    late.append(swap(away, "core"))
    late_units.append(codes_of(units))
    other2, total, *state = lax.optimization_barrier((other2, total, *state))
    units = [(other2, 0, (2, 1, 1))]
    *state, away = stage(units, state, None, last=True)
    late.append(swap(away, "core"))
    late_units.append(codes_of(units))

    share = jnp.pad((total.astype(F32) * token_count ** (-0.5)).astype(BF16), ((0, 16), (0, 0)))
    other_share = swap(share, "replica")
    input_gradient, projected_keys = finish(
        where,
        scale,
        hidden,
        cotangent,
        (3, 1, 1),
        [other3, swap(other3, "core")],
        [state[0], swap(state[1], "core")],
        state[2],
        late,
        late_units,
    )
    weight_gradient = join(where, share, other_share)
    return (projected_keys, input_gradient, weight_gradient, peak_ratio)


def plain(hidden_states, key_weight, previous_peak, key_cotangent):
    names = ("replica", "x", "core")
    limit = previous_peak[0]
    unscale = limit / 448.0
    tokens, width = hidden_states.shape
    rows, features = key_weight.shape
    replicas = lax.axis_size("replica")
    nz, nx, nc = lax.axis_size("z"), lax.axis_size("x"), lax.axis_size("core")
    part = rows // replicas
    group = replicas * nx * nc
    split = hidden_states.reshape(tokens, nz, nx, nc, replicas, part)
    split = split.transpose(4, 2, 3, 0, 1, 5).reshape(group, tokens, nz * part)
    swapped = lax.all_to_all(split, names, 0, 0, tiled=True)
    cotangents = lax.all_gather(key_cotangent, names, axis=0, tiled=True)
    peak = lax.pmax(jnp.max(jnp.abs(key_weight.astype(F32))), ("z", "x", "core"))
    half = lax.dynamic_slice_in_dim(key_weight, lax.axis_index("replica") * part, part, 0)
    gathered = lax.all_gather(
        quantize(half, limit), ("z", "x", "core", "replica"), axis=0, tiled=True
    )
    keys_sum = jnp.dot(hidden_states, gathered, preferred_element_type=F32)
    grad_sum = lax.dot_general(
        key_cotangent, gathered, (((1,), (1,)), ((), ())), preferred_element_type=F32
    )
    term = lax.dot_general(
        swapped.reshape(group * tokens, nz * part),
        cotangents,
        (((0,), (0,)), ((), ())),
        preferred_element_type=F32,
    ).astype(BF16)
    total = lax.psum_scatter(term, "z", scatter_dimension=0, tiled=True).astype(F32)
    token_count = tokens * replicas * nz * nx * nc
    share = (total * token_count ** (-0.5)).astype(BF16)
    weight_gradient = lax.all_gather(share, "replica", axis=0, tiled=True)
    return (
        (keys_sum * unscale).astype(BF16),
        (grad_sum * unscale).astype(BF16),
        weight_gradient,
        (peak / limit).reshape(1),
    )


def solution(mesh):
    replicas, shards = mesh.shape["replica"], mesh.shape["fsdp"]
    grid = Mesh(mesh.devices.reshape(replicas, shards // 4, 2, 2), ("replica", "z", "x", "core"))
    fsdp = ("z", "x", "core")
    every = ("replica",) + fsdp
    in_specs = (P(every, None), P(fsdp, None), P(), P(every, None))
    out_specs = (P(every, None), P(every, None), P(fsdp, None), P())
    run = body if replicas == 2 and shards == 16 else plain
    return jax.shard_map(run, mesh=grid, in_specs=in_specs, out_specs=out_specs, check_vma=False)
```
